512 devices in a mesh: tm: 8 (over z_hi, y), mesh: 64 (over z_lo, x, core).
Axes of the slice: x: 4, y: 4, z: 16 (z_hi: 2, z_lo: 8; z = z_hi * 8 + z_lo), core: 2. Of those that a mesh axis runs over, the one named last changes fastest.
Arguments:
- inverse: bfloat16 [8, 135, 135, 8192], P('tm', None, None, 'mesh'), may hold values from -0.3 to 1.9
- start: float32 [8, 135, 8192], P('tm', None, 'mesh'), may hold values from -6 to 6
- source: float32 [8, 135, 8192], P('tm', None, 'mesh'), may hold values from -6 to 6
- mass: float32 [135, 8192], P(None, 'mesh'), may hold values from 0.1 to 1
- inner_elem: int32 [2, 16384], P(None, 'mesh'), may hold values from 0 to 127
- inner_face: int32 [2, 16384], P(None, 'mesh'), may hold values from 0 to 5
- inner_orient: int32 [16384], P('mesh'), may hold values from 0 to 7
- inner_jac: float32 [8, 2, 25, 16384], P('tm', None, None, 'mesh'), may hold values from -0.72 to 0.72
- cross_elem: int32 [64, 160], P('mesh'), may hold values from 0 to 127
- cross_face: int32 [64, 160], P('mesh'), may hold values from 0 to 5
- cross_orient: int32 [64, 160], P('mesh'), may hold values from 0 to 7, as said below
- cross_count: int32 [64, 5], P('mesh'), may hold values from 1 to 32, as said below
- cross_jac: float32 [8, 25, 64, 160], P('tm', None, 'mesh'), may hold values from -0.72 to 0.72
Outputs:
- adjoint: float32 [8, 135, 8192], P('tm', None, 'mesh')
The draws below stay inside these ranges and needn't reach their ends.
Inputs may be any that keep to these rules, and one draw needn't show every extreme that they name: cross_count[(p + off[k]) mod 64, mirror[k]] = cross_count[p, k], and cross_count[p, 3] = 32. cross_orient[(p + off[k]) mod 64, mirror[k] * 32 + s] = inv(cross_orient[p, k * 32 + s]).
All inputs are finite; a program needn't handle non-finite values.
Results may differ from the reference program's by a relative error of at most 0.008.
Values sent between devices are 32-bit elements; how exact they have to be, the bound alone decides.
No kernel may reach another device: no remote copies, remote signals or barrier semaphores. Data moves between devices by JAX's collectives and lax.ppermute only.
A program may use at most 128 MiB of HBM per device.

```python
import math
import jax
import jax.numpy as jnp
import numpy as np
from jax import lax

BLK = 135
E_DEV = 128
FMAX = 32
SWEEPS = 2
FIN = 256
TIMES = 8
ELEMS = 8192
N_MESH = 64


def inverse_orientations():
    perm_table = np.zeros((8, 9), np.int32)
    for orient in range(8):
        for tangent_v in range(3):
            for tangent_u in range(3):
                moved_u, moved_v = (tangent_v, tangent_u) if orient // 4 else (tangent_u, tangent_v)
                if orient % 2:
                    moved_u = 2 - moved_u
                if orient // 2 % 2:
                    moved_v = 2 - moved_v
                perm_table[orient, 3 * tangent_v + tangent_u] = 3 * moved_v + moved_u
    inverse_table = np.zeros((8,), np.int32)
    for orient in range(8):
        for candidate in range(8):
            if np.all(perm_table[candidate][perm_table[orient]] == np.arange(9)):
                inverse_table[orient] = candidate
    return inverse_table


def draw_inverse(key, part):
    key = jax.random.fold_in(key, 11)
    noise_key, diag_key = jax.random.split(key)
    full_shape = (TIMES, BLK, BLK, ELEMS)
    noise = jnp.clip(jax.random.normal(noise_key, full_shape, jnp.float32), -6.0, 6.0)
    diagonal = jax.random.uniform(diag_key, (TIMES, BLK, 1, ELEMS), jnp.float32, 0.6, 1.4)
    identity = (jnp.arange(BLK)[:, None] == jnp.arange(BLK)[None, :]).astype(jnp.float32)
    return (noise * (0.5 / math.sqrt(BLK)) + identity[None, :, :, None] * diagonal).astype(jnp.bfloat16)


def draw_cross_orient(key, part):
    key = jax.random.fold_in(key, 12)
    raw_orient = jax.random.randint(key, (N_MESH, 5, FMAX), 0, 8, jnp.int32)
    inverse_row = jnp.asarray(inverse_orientations(), jnp.int32)
    half_way = N_MESH // 2
    first = raw_orient[:, 0]
    second = jnp.take(inverse_row, jnp.roll(first, 1, axis=0))
    third = raw_orient[:, 2]
    fifth = jnp.take(inverse_row, jnp.roll(third, half_way - 1, axis=0))
    rows_id = jnp.arange(N_MESH)[:, None]
    fourth = jnp.where(rows_id < half_way, raw_orient[:, 3], jnp.take(inverse_row, jnp.roll(raw_orient[:, 3], half_way, axis=0)))
    return jnp.stack([first, second, third, fourth, fifth], axis=1).reshape(N_MESH, 5 * FMAX).astype(jnp.int32)


def draw_cross_count(key, part):
    key = jax.random.fold_in(key, 13)
    raw_count = jax.random.randint(key, (N_MESH, 5), 1, FMAX + 1, jnp.int32)
    half_way = N_MESH // 2
    first = raw_count[:, 0]
    second = jnp.roll(first, 1)
    third = raw_count[:, 2]
    fifth = jnp.roll(third, half_way - 1)
    fourth = jnp.full((N_MESH,), FMAX, jnp.int32)
    return jnp.stack([first, second, third, fourth, fifth], axis=1).astype(jnp.int32)


def with_ends(result, key, smallest, largest):
    shape = result.shape
    spot = [jax.random.randint(jax.random.fold_in(key, axis), (), 0, shape[axis]) for axis in range(len(shape))]
    result = result.at[tuple(spot)].set(smallest)
    longest = shape.index(max(shape))
    spot[longest] = (spot[longest] + 1) % shape[longest]
    return result.at[tuple(spot)].set(largest)


def steps_of(key, extent, cuts, least, largest):
    def one(position, blocks):
        steps = jax.random.uniform(jax.random.fold_in(jax.random.fold_in(key, 6), position), (blocks,), jnp.float32, least / len(cuts), largest / len(cuts))
        return jnp.repeat(jnp.exp(steps), extent[position] // blocks).reshape((-1,) + (1,) * (len(extent) - position - 1))

    level = one(*cuts[0])
    for cut in cuts[1:]:
        level = level * one(*cut)
    return level


def bell_draw(stream_key, shape, spread, most, shards=(), kind=jnp.bfloat16):
    entries = jax.random.normal(stream_key, shape, jnp.float32) * spread
    if len(shards) > 0:
        entries = steps_of(stream_key, shape, shards, -0.22, 0.18) * entries
    return jnp.clip(entries, min=-most, max=most).astype(kind)


def setup_inputs(seed: int = 0) -> dict:
    key_of = jax.random.split(jax.random.key(seed), 14)
    return {
        "inverse": draw_inverse(jax.random.fold_in(key_of[13], 71), 0),
        "start": bell_draw(key_of[1], (TIMES, BLK, ELEMS), 1.0, 6.0, ((0, 8), (2, 64)), jnp.float32),
        "source": bell_draw(key_of[2], (TIMES, BLK, ELEMS), 1.0, 6.0, ((0, 8), (2, 64)), jnp.float32),
        "mass": jnp.clip(jnp.exp(math.log(1.0) - 2.3025851 * jax.random.uniform(key_of[3], (BLK, ELEMS), jnp.float32) ** steps_of(key_of[3], (BLK, ELEMS), ((1, 64),), -0.2, 0.2)), 0.1, 1.0),
        "inner_elem": with_ends(jax.random.randint(key_of[4], (2, N_MESH * FIN), 0, E_DEV), jax.random.fold_in(key_of[4], 1), 0, E_DEV - 1).astype(jnp.int32),
        "inner_face": with_ends(jax.random.randint(key_of[5], (2, N_MESH * FIN), 0, 6), jax.random.fold_in(key_of[5], 1), 0, 5).astype(jnp.int32),
        "inner_orient": with_ends(jax.random.randint(key_of[6], (N_MESH * FIN,), 0, 8), jax.random.fold_in(key_of[6], 1), 0, 7).astype(jnp.int32),
        "inner_jac": bell_draw(key_of[7], (TIMES, 2, 25, N_MESH * FIN), 0.12, 0.72, ((0, 8), (3, 64)), jnp.float32),
        "cross_elem": with_ends(jax.random.randint(key_of[8], (N_MESH, 5 * FMAX), 0, E_DEV), jax.random.fold_in(key_of[8], 1), 0, E_DEV - 1).astype(jnp.int32),
        "cross_face": with_ends(jax.random.randint(key_of[9], (N_MESH, 5 * FMAX), 0, 6), jax.random.fold_in(key_of[9], 1), 0, 5).astype(jnp.int32),
        "cross_orient": draw_cross_orient(jax.random.fold_in(key_of[13], 71), 0),
        "cross_count": draw_cross_count(jax.random.fold_in(key_of[13], 71), 0),
        "cross_jac": bell_draw(key_of[12], (TIMES, 25, N_MESH, 5 * FMAX), 0.12, 0.72, ((0, 8), (2, 64)), jnp.float32),
    }


line_weights = (1.0 / 3.0, 4.0 / 3.0, 1.0 / 3.0)
highest = lax.Precision.HIGHEST
mirror_list = (1, 0, 4, 3, 2)


def build_tables():
    face_nodes = np.zeros((6, 9), np.int32)
    face_weight = np.zeros((9,), np.float32)
    for face_index in range(6):
        normal_axis = face_index // 2
        tangent_axes = [other_axis for other_axis in range(3) if other_axis != normal_axis]
        for tangent_v in range(3):
            for tangent_u in range(3):
                coords = [0, 0, 0]
                coords[normal_axis] = 2 * (face_index % 2)
                coords[tangent_axes[0]] = tangent_u
                coords[tangent_axes[1]] = tangent_v
                face_nodes[face_index, 3 * tangent_v + tangent_u] = 9 * coords[2] + 3 * coords[1] + coords[0]
                face_weight[3 * tangent_v + tangent_u] = line_weights[tangent_u] * line_weights[tangent_v]
    perm_table = np.zeros((8, 9), np.int32)
    for orient in range(8):
        for tangent_v in range(3):
            for tangent_u in range(3):
                moved_u, moved_v = (tangent_v, tangent_u) if orient // 4 else (tangent_u, tangent_v)
                if orient % 2:
                    moved_u = 2 - moved_u
                if (orient // 2) % 2:
                    moved_v = 2 - moved_v
                perm_table[orient, 3 * tangent_v + tangent_u] = 3 * moved_v + moved_u
    inverse_table = np.zeros((8,), np.int32)
    for orient in range(8):
        for candidate in range(8):
            if np.all(perm_table[candidate][perm_table[orient]] == np.arange(9)):
                inverse_table[orient] = candidate
    return face_nodes, face_weight, perm_table, inverse_table


def time_matrix(count_times):
    table = [0.0] * count_times
    for offset in range(1, count_times):
        parity = (-1.0) ** offset
        phase = math.pi * offset / count_times
        table[offset] = 0.3 * parity * math.cos(phase) / math.sin(phase) + 1.2 * parity / count_times
    matrix = [[table[(col_index - row_index) % count_times] for col_index in range(count_times)] for row_index in range(count_times)]
    return np.array(matrix, np.float32)


def couple(state, jacobian, send_col, send_face, recv_col, recv_face, orients, live):
    face_nodes, face_weight, perm_table, inverse_table = build_tables()
    node_table = jnp.asarray(face_nodes)
    slot_total = send_col.shape[0]
    gathered = state[:, send_col].reshape(5, 27, slot_total)
    send_nodes = node_table[send_face].T
    trace = jnp.take_along_axis(gathered, send_nodes[None], axis=1) * jnp.asarray(face_weight)[None, :, None]
    perm_rows = jnp.asarray(perm_table)[orients].T
    permuted = jnp.take_along_axis(trace, perm_rows[None], axis=1)
    received = jnp.einsum('uvs,uns->vns', jacobian.reshape(5, 5, slot_total), permuted, precision=highest)
    received = jnp.where(live[None, None, :], received, 0.0)
    recv_nodes = node_table[recv_face].T
    total = jnp.zeros((5, 27, state.shape[1]), jnp.float32)
    total = total.at[:, recv_nodes, recv_col[None, :]].add(received)
    return total.reshape(BLK, state.shape[1])


def reference(inverse, start, source, mass, inner_elem, inner_face, inner_orient, inner_jac, cross_elem, cross_face, cross_orient, cross_count, cross_jac):
    face_nodes, face_weight, perm_table, inverse_table = build_tables()
    parts = N_MESH
    inner_base = (jnp.arange(parts * FIN, dtype=jnp.int32) // FIN) * E_DEV
    column_a = inner_base + inner_elem[0]
    column_b = inner_base + inner_elem[1]
    back_orient = jnp.asarray(inverse_table)[inner_orient].astype(jnp.int32)
    offsets = jnp.asarray([1, parts - 1, parts // 2 - 1, parts // 2, parts // 2 + 1], jnp.int32)
    mirror = jnp.asarray(mirror_list, jnp.int32)
    cube_elem = cross_elem.reshape(parts, 5, FMAX)
    cube_face = cross_face.reshape(parts, 5, FMAX)
    part_index = jnp.arange(parts, dtype=jnp.int32)
    partner = ((part_index[:, None] + offsets[None, :]) % parts).astype(jnp.int32)
    mirror_grid = jnp.broadcast_to(mirror[None, :], (parts, 5))
    send_elem = cube_elem[partner, mirror_grid]
    send_face_cube = cube_face[partner, mirror_grid]
    recv_cross = (part_index[:, None, None] * E_DEV + cube_elem).reshape(-1)
    send_cross = (partner[:, :, None] * E_DEV + send_elem).reshape(-1)
    slot_index = jnp.arange(FMAX, dtype=jnp.int32)
    live_cross = (slot_index[None, None, :] < cross_count[:, :, None]).reshape(-1)
    send_col = jnp.concatenate([column_b, column_a, send_cross]).astype(jnp.int32)
    send_face = jnp.concatenate([inner_face[1], inner_face[0], send_face_cube.reshape(-1)]).astype(jnp.int32)
    recv_col = jnp.concatenate([column_a, column_b, recv_cross]).astype(jnp.int32)
    recv_face = jnp.concatenate([inner_face[0], inner_face[1], cross_face.reshape(-1)]).astype(jnp.int32)
    orients = jnp.concatenate([inner_orient, back_orient, cross_orient.reshape(-1)]).astype(jnp.int32)
    live = jnp.concatenate([jnp.ones((2 * parts * FIN,), bool), live_cross])
    jac_all = jnp.concatenate([inner_jac[:, 0], inner_jac[:, 1], cross_jac.reshape(TIMES, 25, -1)], axis=2)
    matrix = jnp.asarray(time_matrix(TIMES))
    current = start
    for sweep_index in range(SWEEPS):
        coupling = lax.map(lambda operands: couple(operands[0], operands[1], send_col, send_face, recv_col, recv_face, orients, live), (current, jac_all))
        spectral = jnp.einsum('ts,sie->tie', matrix, current, precision=highest)
        resid = (source - coupling - mass[None] * spectral).astype(jnp.bfloat16)
        current = lax.map(lambda operands: jnp.einsum('ije,je->ie', operands[0].astype(jnp.float32), operands[1].astype(jnp.float32), precision=highest), (inverse, resid))
    return current
```

```python
import functools
import math

import jax
import jax.numpy as jnp
import numpy as np
from jax import lax
from jax.experimental import pallas as pl
from jax.experimental.pallas import tpu as pltpu
from jax.sharding import PartitionSpec as P

SWEEPS = 2
LINE = (1.0 / 3.0, 4.0 / 3.0, 1.0 / 3.0)
CHUNKS = 9
VMEM = pl.BlockSpec(memory_space=pltpu.VMEM)
SMEM = pl.BlockSpec(memory_space=pltpu.SMEM)


def face_node(face, n):
    normal = face // 2
    tangent = [axis for axis in range(3) if axis != normal]
    coords = [0, 0, 0]
    coords[normal] = 2 * (face % 2)
    coords[tangent[0]] = n % 3
    coords[tangent[1]] = n // 3
    return 9 * coords[2] + 3 * coords[1] + coords[0]


NODE = [[face_node(face, n) for n in range(9)] for face in range(6)]
WEIGHT = [float(np.float32(LINE[n % 3] * LINE[n // 3])) for n in range(9)]


def coef_table(times):
    table = [0.0] * times
    for k in range(1, times):
        sign = (-1.0) ** k
        phase = math.pi * k / times
        table[k] = float(
            np.float32(0.3 * sign * math.cos(phase) / math.sin(phase) + 1.2 * sign / times)
        )
    return table


def split_rows(value):
    high = value.astype(jnp.bfloat16).astype(jnp.float32)
    return jnp.concatenate([high, value - high], axis=0).astype(jnp.bfloat16)


def join_rows(value):
    half = value.shape[0] // 2
    return value[:half] + value[half:]


def face_rows(x_ref):
    elems = x_ref.shape[1]
    pad = jnp.zeros((3, elems), jnp.float32)
    nodes = [
        jnp.concatenate([x_ref[pl.ds(m, 5, stride=27), :], pad], axis=0) for m in range(27)
    ]
    blocks = []
    for face in range(6):
        rows = jnp.concatenate([nodes[NODE[face][n]] * WEIGHT[n] for n in range(9)], axis=0)
        blocks.append(split_rows(rows))
    return jnp.concatenate(blocks, axis=1)


def onehot(code, elems):
    slots = code.shape[1]
    row = lax.broadcasted_iota(jnp.int32, (elems, slots), 0)
    parts = [
        jnp.where(row == code - face * elems, 1.0, 0.0).astype(jnp.bfloat16) for face in range(6)
    ]
    return jnp.concatenate(parts, axis=0)


def cross_code(elem_ref, face_ref, elems, order):
    code = face_ref[...] * elems + elem_ref[...]
    cap = code.shape[1] // 5
    parts = [code[:, k * cap : (k + 1) * cap] for k in order]
    fill = 256 - code.shape[1]
    return jnp.concatenate(parts + [jnp.full((1, fill), -1, jnp.int32)], axis=1)


def cross_trace(x_ref, elem_ref, face_ref, near_ref, far_ref):
    hot = onehot(cross_code(elem_ref, face_ref, x_ref.shape[1], (0, 4, 1, 2, 3)), x_ref.shape[1])
    trace = join_rows(jnp.dot(face_rows(x_ref), hot, preferred_element_type=jnp.float32))
    near_ref[...] = trace[:, :128]
    far_ref[...] = trace[:, 128:]


def received_rows(trace, orient, jacobian):
    slots = trace.shape[1]
    code = jnp.broadcast_to(orient, (8, slots))
    flip_i = (code & 1) == 1
    flip_j = ((code >> 1) & 1) == 1
    swap = code >= 4
    tile = [trace[8 * n : 8 * n + 8] for n in range(9)]
    for j in range(3):
        low, high = tile[3 * j], tile[3 * j + 2]
        tile[3 * j] = jnp.where(flip_i, high, low)
        tile[3 * j + 2] = jnp.where(flip_i, low, high)
    for i in range(3):
        low, high = tile[i], tile[6 + i]
        tile[i] = jnp.where(flip_j, high, low)
        tile[6 + i] = jnp.where(flip_j, low, high)
    for j in range(3):
        for i in range(j):
            one, two = tile[3 * j + i], tile[3 * i + j]
            tile[3 * j + i] = jnp.where(swap, two, one)
            tile[3 * i + j] = jnp.where(swap, one, two)
    rows = []
    for n in range(9):
        total = jacobian[0] * tile[n][0:1]
        for u in range(1, 5):
            total = total + jacobian[u] * tile[n][u : u + 1]
        rows.append(total)
    return jnp.concatenate(rows, axis=0)


def scatter_nodes(rows, hot, elems):
    placed = join_rows(
        lax.dot_general(
            split_rows(rows), hot, (((1,), (1,)), ((), ())), preferred_element_type=jnp.float32
        )
    )
    nodes = [None] * 27
    for face in range(6):
        for n in range(9):
            part = placed[8 * n : 8 * n + 8, face * elems : (face + 1) * elems]
            m = NODE[face][n]
            nodes[m] = part if nodes[m] is None else nodes[m] + part
    return nodes


def inner_kernel(x_ref, elem_ref, face_ref, orient_ref, jac_ref, out_ref):
    elems = x_ref.shape[1]
    half = elem_ref.shape[1]
    code = face_ref[...] * elems + elem_ref[...]
    hot = onehot(jnp.concatenate([code[0:1], code[1:2]], axis=1), elems)
    trace = join_rows(jnp.dot(face_rows(x_ref), hot, preferred_element_type=jnp.float32))
    trace = jnp.concatenate([trace[:, half:], trace[:, :half]], axis=1)
    orient = orient_ref[...]
    back = jnp.where(orient >= 4, 4 + 2 * (orient & 1) + ((orient >> 1) & 1), orient)
    pad = jnp.zeros((3, 2 * half), jnp.float32)
    jacobian = []
    for u in range(5):
        rows = jnp.concatenate(
            [jac_ref[0, side, 5 * u : 5 * u + 5, :] for side in range(2)], axis=1
        )
        jacobian.append(jnp.concatenate([rows, pad], axis=0))
    rows = received_rows(trace, jnp.concatenate([orient, back], axis=1), jacobian)
    nodes = scatter_nodes(rows, hot, elems)
    for m in range(27):
        out_ref[8 * m : 8 * m + 8, :] = (
            nodes[m] if nodes[m] is not None else jnp.zeros((8, elems), jnp.float32)
        )


def combine_kernel(times, x_ref, z_ref, one_ref, two_ref, three_ref):
    table = coef_table(times)
    half = times // 2
    y = lax.axis_index("tm") % half
    x = x_ref[...]
    z = z_ref[...]
    for step, out in ((1, one_ref), (2, two_ref), (3, three_ref)):
        wraps = y + step >= half
        first = table[times - step]
        second = table[half - step]
        out[...] = x * jnp.where(wraps, second, first) + z * jnp.where(wraps, first, second)


def relay_kernel(cap, even_ref, odd_ref, far_ref, out_ref):
    is_even = lax.axis_index("mesh") % 2 == 0
    even = even_ref[...]
    odd = odd_ref[...]
    above = jnp.where(is_even, even, odd)
    below = jnp.where(is_even, odd, even)
    out_ref[...] = jnp.concatenate(
        [far_ref[:, :cap], below[:, cap : 2 * cap], above[:, 3 * cap : 4 * cap], far_ref[:, :cap]],
        axis=1,
    )


def final_kernel(
    cap,
    last,
    table_half,
    inner_ref,
    even_ref,
    odd_ref,
    far_ref,
    elem_ref,
    face_ref,
    orient_ref,
    count_ref,
    jac_ref,
    source_ref,
    mass_ref,
    z_ref,
    one_ref,
    two_ref,
    three_ref,
    inverse_ref,
    *rest,
):
    if last:
        out_ref, resid_ref, held_ref, sems = rest
    else:
        out_ref, near_ref, send_ref, resid_ref, held_ref, sems = rest
    size, elems = source_ref.shape
    per = size // CHUNKS
    copies = []
    for c in range(CHUNKS):
        copy = pltpu.make_async_copy(
            inverse_ref.at[0, pl.ds(c * per, per)], held_ref.at[pl.ds(c * per, per)], sems.at[c]
        )
        copy.start()
        copies.append(copy)

    is_even = lax.axis_index("mesh") % 2 == 0
    even = even_ref[...]
    odd = odd_ref[...]
    far = far_ref[...]
    above = jnp.where(is_even, even, odd)
    below = jnp.where(is_even, odd, even)
    slots = 5 * cap
    fill = 256 - slots
    trace = jnp.concatenate(
        [
            above[:, 2 * cap : 3 * cap],
            below[:, :cap],
            far[:, cap : 2 * cap],
            far[:, :cap],
            far[:, 2 * cap : 3 * cap],
            jnp.zeros((72, fill), jnp.float32),
        ],
        axis=1,
    )
    hot = onehot(cross_code(elem_ref, face_ref, elems, range(5)), elems)
    orient = jnp.concatenate([orient_ref[...], jnp.zeros((1, fill), jnp.int32)], axis=1)
    lane = lax.broadcasted_iota(jnp.int32, (8, 256), 1)
    live = lane < 0
    for k in range(5):
        live = live | ((lane >= k * cap) & (lane < k * cap + count_ref[0, k]))
    jacobian = []
    for u in range(5):
        rows = jnp.concatenate(
            [jac_ref[5 * u : 5 * u + 5, :], jnp.zeros((5, fill), jnp.float32)], axis=1
        )
        rows = jnp.concatenate([rows, jnp.zeros((3, 256), jnp.float32)], axis=0)
        jacobian.append(jnp.where(live, rows, 0.0))
    nodes = scatter_nodes(received_rows(trace, orient, jacobian), hot, elems)
    for m in range(27):
        part = inner_ref[8 * m : 8 * m + 8, :]
        part = part if nodes[m] is None else part + nodes[m]
        resid_ref[pl.ds(m, 5, stride=27), :] = part[:5]
    spectral = z_ref[...] * table_half + one_ref[...] + two_ref[...] + three_ref[...]
    resid = source_ref[...] - resid_ref[...] - mass_ref[...] * spectral
    resid = resid.astype(jnp.bfloat16).astype(jnp.float32)
    for c in range(CHUNKS):
        copies[c].wait()

        def body(step, carry):
            for r in range(5):
                i = c * per + step * 5 + r
                product = held_ref[i].astype(jnp.float32) * resid
                out_ref[pl.ds(i, 1), :] = jnp.sum(product, axis=0, keepdims=True)
            return carry

        lax.fori_loop(0, per // 5, body, 0)
    if not last:
        cross_trace(out_ref, elem_ref, face_ref, near_ref, send_ref)


def on_device(
    inverse,
    start,
    source,
    mass,
    inner_elem,
    inner_face,
    inner_orient,
    inner_jac,
    cross_elem,
    cross_face,
    cross_orient,
    cross_count,
    cross_jac,
):
    size, elems = start.shape[1:]
    count_mesh = lax.axis_size("mesh")
    times = lax.axis_size("tm")
    half_times = times // 2
    cap = cross_elem.shape[1] // 5
    table = coef_table(times)
    f32 = jnp.float32
    state = jax.ShapeDtypeStruct((size, elems), f32)
    near_shape = jax.ShapeDtypeStruct((72, 128), f32)
    params = pltpu.CompilerParams(vmem_limit_bytes=40 * 1024 * 1024)

    across = [(t, (t + half_times) % times) for t in range(times)]
    around = [
        [(t, t // half_times * half_times + (t + step) % half_times) for t in range(times)]
        for step in (1, 2, 3)
    ]
    evens = [(p, p ^ 1) for p in range(count_mesh)]
    odds = [(p, ((p + 1) ^ 1) - 1) for p in range(count_mesh)]
    odds = [(p, q % count_mesh) for p, q in odds]
    opposite = [(p, (p + count_mesh // 2) % count_mesh) for p in range(count_mesh)]

    x = start[0]
    source = source[0]
    orient_row = inner_orient[None, :]
    jac_row = cross_jac[0, :, 0, :]
    near, far = pl.pallas_call(
        cross_trace,
        out_shape=(near_shape, near_shape),
        in_specs=[VMEM] * 3,
        out_specs=(VMEM, VMEM),
        compiler_params=params,
    )(x, cross_elem, cross_face)
    for sweep in range(SWEEPS):
        last = sweep == SWEEPS - 1
        over = lax.ppermute(x, "tm", across)
        even = lax.ppermute(near, "mesh", evens)
        odd = lax.ppermute(near, "mesh", odds)
        inner = pl.pallas_call(
            inner_kernel,
            out_shape=jax.ShapeDtypeStruct((216, elems), f32),
            in_specs=[VMEM] * 5,
            out_specs=VMEM,
            compiler_params=params,
        )(x, inner_elem, inner_face, orient_row, inner_jac)
        parts = pl.pallas_call(
            functools.partial(combine_kernel, times),
            out_shape=(state,) * 3,
            in_specs=[VMEM] * 2,
            out_specs=(VMEM,) * 3,
            compiler_params=params,
        )(x, over)
        parts = [lax.ppermute(part, "tm", pairs) for part, pairs in zip(parts, around)]
        passed = pl.pallas_call(
            functools.partial(relay_kernel, cap),
            out_shape=near_shape,
            in_specs=[VMEM] * 3,
            out_specs=VMEM,
            compiler_params=params,
        )(even, odd, far)
        passed = lax.ppermute(passed, "mesh", opposite)
        result = pl.pallas_call(
            functools.partial(final_kernel, cap, last, table[half_times]),
            out_shape=(state,) if last else (state, near_shape, near_shape),
            in_specs=[VMEM] * 7 + [SMEM] + [VMEM] * 7 + [pl.BlockSpec(memory_space=pl.ANY)],
            out_specs=(VMEM,) if last else (VMEM,) * 3,
            scratch_shapes=[
                pltpu.VMEM((size, elems), f32),
                pltpu.VMEM((size, size, elems), jnp.bfloat16),
                pltpu.SemaphoreType.DMA((CHUNKS,)),
            ],
            compiler_params=params,
        )(
            inner,
            even,
            odd,
            passed,
            cross_elem,
            cross_face,
            cross_orient,
            cross_count,
            jac_row,
            source,
            mass,
            over,
            *parts,
            inverse,
        )
        if last:
            return result[0][None]
        x, near, far = result


def solution(mesh):
    in_specs = (
        P("tm", None, None, "mesh"),
        P("tm", None, "mesh"),
        P("tm", None, "mesh"),
        P(None, "mesh"),
        P(None, "mesh"),
        P(None, "mesh"),
        P("mesh"),
        P("tm", None, None, "mesh"),
        P("mesh", None),
        P("mesh", None),
        P("mesh", None),
        P("mesh", None),
        P("tm", None, "mesh", None),
    )
    out_specs = P("tm", None, "mesh")
    return jax.shard_map(
        on_device, mesh=mesh, in_specs=in_specs, out_specs=out_specs, check_vma=False
    )
```

```python
import functools
import math

import jax
import jax.numpy as jnp
import numpy as np
from jax import lax
from jax.experimental import pallas as pl
from jax.experimental.pallas import tpu as pltpu
from jax.sharding import PartitionSpec as P

SWEEPS = 2
LINE = (1.0 / 3.0, 4.0 / 3.0, 1.0 / 3.0)
VMEM = pl.BlockSpec(memory_space=pltpu.VMEM)
HBM = pl.BlockSpec(memory_space=pltpu.HBM)


def face_node(face, n):
    normal = face // 2
    tangent = [axis for axis in range(3) if axis != normal]
    coords = [0, 0, 0]
    coords[normal] = 2 * (face % 2)
    coords[tangent[0]] = n % 3
    coords[tangent[1]] = n // 3
    return 9 * coords[2] + 3 * coords[1] + coords[0]


NODE = [[face_node(face, n) for n in range(9)] for face in range(6)]
WEIGHT = [float(np.float32(LINE[n % 3] * LINE[n // 3])) for n in range(9)]


def coef_table(times):
    table = [0.0] * times
    for k in range(1, times):
        sign = (-1.0) ** k
        phase = math.pi * k / times
        table[k] = float(
            np.float32(0.3 * sign * math.cos(phase) / math.sin(phase) + 1.2 * sign / times)
        )
    return table


def split_rows(value):
    high = value.astype(jnp.bfloat16).astype(jnp.float32)
    return jnp.concatenate([high, value - high], axis=0).astype(jnp.bfloat16)


def join_rows(value):
    half = value.shape[0] // 2
    return value[:half] + value[half:]


def face_rows(x_ref):
    elems = x_ref.shape[1]
    pad = jnp.zeros((3, elems), jnp.float32)
    nodes = [
        jnp.concatenate([x_ref[pl.ds(m, 5, stride=27), :], pad], axis=0) for m in range(27)
    ]
    blocks = []
    for face in range(6):
        rows = jnp.concatenate([nodes[NODE[face][n]] * WEIGHT[n] for n in range(9)], axis=0)
        blocks.append(split_rows(rows))
    return jnp.concatenate(blocks, axis=1)


def onehot(code, elems):
    slots = code.shape[1]
    row = lax.broadcasted_iota(jnp.int32, (elems, slots), 0)
    parts = [
        jnp.where(row == code - face * elems, 1.0, 0.0).astype(jnp.bfloat16) for face in range(6)
    ]
    return jnp.concatenate(parts, axis=0)


def cross_code(elem_ref, face_ref, elems, order):
    code = face_ref[...] * elems + elem_ref[...]
    cap = code.shape[1] // 5
    parts = [code[:, k * cap : (k + 1) * cap] for k in order]
    fill = 256 - code.shape[1]
    return jnp.concatenate(parts + [jnp.full((1, fill), -1, jnp.int32)], axis=1)


def cross_trace(x_ref, hot, near_ref, far_ref):
    trace = join_rows(jnp.dot(face_rows(x_ref), hot, preferred_element_type=jnp.float32))
    near_ref[...] = trace[:, :128]
    far_ref[...] = trace[:, 128:]


def fetch(pairs, sems):
    copies = [
        pltpu.make_async_copy(source, target, sems.at[i])
        for i, (source, target) in enumerate(pairs)
    ]
    for copy in copies:
        copy.start()
    return copies


def first_kernel(
    start_ref, elem_hbm, face_hbm, x_ref, near_ref, far_ref, hot_ref, elem_ref, face_ref, sems
):
    copies = fetch(
        ((start_ref.at[:, 0], x_ref), (elem_hbm, elem_ref), (face_hbm, face_ref)), sems
    )
    for copy in copies[1:]:
        copy.wait()
    elems = x_ref.shape[1]
    hot_ref[...] = onehot(cross_code(elem_ref, face_ref, elems, (0, 4, 1, 2, 3)), elems)
    copies[0].wait()
    cross_trace(x_ref, hot_ref[...], near_ref, far_ref)


def received_rows(trace, orient, jacobian):
    slots = trace.shape[1]
    code = jnp.broadcast_to(orient, (8, slots))
    flip_i = (code & 1) == 1
    flip_j = ((code >> 1) & 1) == 1
    swap = code >= 4
    tile = [trace[8 * n : 8 * n + 8] for n in range(9)]
    for j in range(3):
        low, high = tile[3 * j], tile[3 * j + 2]
        tile[3 * j] = jnp.where(flip_i, high, low)
        tile[3 * j + 2] = jnp.where(flip_i, low, high)
    for i in range(3):
        low, high = tile[i], tile[6 + i]
        tile[i] = jnp.where(flip_j, high, low)
        tile[6 + i] = jnp.where(flip_j, low, high)
    for j in range(3):
        for i in range(j):
            one, two = tile[3 * j + i], tile[3 * i + j]
            tile[3 * j + i] = jnp.where(swap, two, one)
            tile[3 * i + j] = jnp.where(swap, one, two)
    rows = []
    for n in range(9):
        total = jacobian[0] * tile[n][0:1]
        for u in range(1, 5):
            total = total + jacobian[u] * tile[n][u : u + 1]
        rows.append(total)
    return jnp.concatenate(rows, axis=0)


def scatter_nodes(rows, hot, elems):
    placed = join_rows(
        lax.dot_general(
            split_rows(rows), hot, (((1,), (1,)), ((), ())), preferred_element_type=jnp.float32
        )
    )
    nodes = [None] * 27
    for face in range(6):
        for n in range(9):
            part = placed[8 * n : 8 * n + 8, face * elems : (face + 1) * elems]
            m = NODE[face][n]
            nodes[m] = part if nodes[m] is None else nodes[m] + part
    return nodes


def inner_sum(x_ref, hot, orient, jac_ref, out_ref):
    elems = x_ref.shape[1]
    half = hot.shape[1] // 2
    trace = join_rows(jnp.dot(face_rows(x_ref), hot, preferred_element_type=jnp.float32))
    trace = jnp.concatenate([trace[:, half:], trace[:, :half]], axis=1)
    jacobian = [jac_ref[8 * u : 8 * u + 8, :] for u in range(5)]
    nodes = scatter_nodes(received_rows(trace, orient, jacobian), hot, elems)
    for m in range(27):
        out_ref[8 * m : 8 * m + 8, :] = (
            nodes[m] if nodes[m] is not None else jnp.zeros((8, elems), jnp.float32)
        )


def prepare_kernel(
    cap,
    x_ref,
    elem_hbm,
    face_hbm,
    orient_hbm,
    jac_hbm,
    cross_elem_hbm,
    cross_face_hbm,
    cross_orient_hbm,
    count_hbm,
    cross_jac_hbm,
    source_hbm,
    mass_hbm,
    out_ref,
    hot_ref,
    turn_ref,
    jac_ref,
    cross_hot_ref,
    cross_turn_ref,
    cross_jac_ref,
    source_ref,
    mass_ref,
    elem_ref,
    face_ref,
    orient_ref,
    raw_ref,
    cross_elem_ref,
    cross_face_ref,
    cross_orient_ref,
    count_ref,
    cross_raw_ref,
    sems,
):
    copies = fetch(
        (
            (elem_hbm, elem_ref),
            (face_hbm, face_ref),
            (orient_hbm, orient_ref),
            (jac_hbm, raw_ref),
            (cross_elem_hbm, cross_elem_ref),
            (cross_face_hbm, cross_face_ref),
            (cross_orient_hbm, cross_orient_ref),
            (count_hbm, count_ref),
            (cross_jac_hbm, cross_raw_ref),
            (source_hbm.at[:, 0], source_ref),
            (mass_hbm, mass_ref),
        ),
        sems,
    )
    for copy in copies:
        copy.wait()
    elems = x_ref.shape[1]
    half = elem_ref.shape[1]
    code = face_ref[...] * elems + elem_ref[...]
    hot_ref[...] = onehot(jnp.concatenate([code[0:1], code[1:2]], axis=1), elems)
    orient = orient_ref[...]
    back = jnp.where(orient >= 4, 4 + 2 * (orient & 1) + ((orient >> 1) & 1), orient)
    turn_ref[...] = jnp.concatenate([orient, back], axis=1)
    jac_ref[...] = jnp.zeros_like(jac_ref)
    for u in range(5):
        for v in range(5):
            for side in range(2):
                jac_ref[8 * u + v : 8 * u + v + 1, side * half : (side + 1) * half] = raw_ref[
                    0, 5 * u + v, side : side + 1, :
                ]
    slots = 5 * cap
    fill = 256 - slots
    cross_hot_ref[...] = onehot(
        cross_code(cross_elem_ref, cross_face_ref, elems, range(5)), elems
    )
    cross_turn_ref[...] = jnp.concatenate(
        [cross_orient_ref[...], jnp.zeros((1, fill), jnp.int32)], axis=1
    )
    lane = lax.broadcasted_iota(jnp.int32, (1, slots), 1)
    count = count_ref[...]
    live = lane < 0
    for k in range(5):
        live = live | ((lane >= k * cap) & (lane - k * cap < count[:, k : k + 1]))
    cross_jac_ref[...] = jnp.zeros_like(cross_jac_ref)
    for u in range(5):
        for v in range(5):
            row = cross_raw_ref[5 * u + v]
            cross_jac_ref[8 * u + v : 8 * u + v + 1, :slots] = jnp.where(live, row, 0.0)
    inner_sum(x_ref, hot_ref[...], turn_ref[...], jac_ref, out_ref)


def inner_kernel(x_ref, hot_ref, turn_ref, jac_ref, out_ref):
    inner_sum(x_ref, hot_ref[...], turn_ref[...], jac_ref, out_ref)


def combine_kernel(times, x_ref, z_ref, out_ref):
    table = coef_table(times)
    half = times // 2
    y = lax.axis_index("tm") % half
    x = x_ref[...]
    z = z_ref[...] if len(z_ref.shape) == 2 else z_ref[:, 0, :]
    for target in range(half):
        own = jnp.float32(0.0)
        other = jnp.float32(0.0)
        for at in range(half):
            own = jnp.where(y == at, table[(at - target) % times], own)
            other = jnp.where(y == at, table[(at - target + half) % times], other)
        out_ref[target] = x * own + z * other


def relay_kernel(cap, even_ref, odd_ref, far_ref, out_ref):
    is_even = lax.axis_index("mesh") % 2 == 0
    even = even_ref[...]
    odd = odd_ref[...]
    above = jnp.where(is_even, even, odd)
    below = jnp.where(is_even, odd, even)
    out_ref[...] = jnp.concatenate(
        [far_ref[:, :cap], below[:, cap : 2 * cap], above[:, 3 * cap : 4 * cap], far_ref[:, :cap]],
        axis=1,
    )


def solve(held_ref, resid, out_ref, first, count):
    def body(step, carry):
        for r in range(5):
            i = first + step * 5 + r
            product = held_ref[0, i].astype(jnp.float32) * resid
            out_ref[pl.ds(i, 1), :] = jnp.sum(product, axis=0, keepdims=True)
        return carry

    lax.fori_loop(0, count // 5, body, 0)


def residual(
    cap,
    inner_ref,
    even_ref,
    odd_ref,
    far_ref,
    hot_ref,
    turn_ref,
    jac_ref,
    source_ref,
    mass_ref,
    terms_ref,
    resid_ref,
):
    elems = source_ref.shape[1]
    is_even = lax.axis_index("mesh") % 2 == 0
    even = even_ref[...]
    odd = odd_ref[...]
    far = far_ref[...]
    above = jnp.where(is_even, even, odd)
    below = jnp.where(is_even, odd, even)
    trace = jnp.concatenate(
        [
            above[:, 2 * cap : 3 * cap],
            below[:, :cap],
            far[:, cap : 2 * cap],
            far[:, :cap],
            far[:, 2 * cap : 3 * cap],
            jnp.zeros((72, 256 - 5 * cap), jnp.float32),
        ],
        axis=1,
    )
    jacobian = [jac_ref[8 * u : 8 * u + 8, :] for u in range(5)]
    nodes = scatter_nodes(received_rows(trace, turn_ref[...], jacobian), hot_ref[...], elems)
    for m in range(27):
        part = inner_ref[8 * m : 8 * m + 8, :]
        part = part if nodes[m] is None else part + nodes[m]
        resid_ref[pl.ds(m, 5, stride=27), :] = part[:5]
    spectral = (terms_ref[0] + terms_ref[1]) + (terms_ref[2] + terms_ref[3])
    resid = source_ref[...] - resid_ref[...] - mass_ref[...] * spectral
    return resid.astype(jnp.bfloat16).astype(jnp.float32)


def middle_kernel(cap, *refs):
    *operands, held_ref, send_ref, out_ref, near_ref, far_ref, resid_ref = refs
    resid = residual(cap, *operands, resid_ref)
    solve(held_ref, resid, out_ref, 0, held_ref.shape[1])
    cross_trace(out_ref, send_ref[...], near_ref, far_ref)


def last_kernel(cap, *refs):
    *operands, held_ref, result_ref, resid_ref, out_ref, sems = refs
    resid = residual(cap, *operands, resid_ref)
    per = held_ref.shape[1] // 3
    copies = []
    for c in range(3):
        solve(held_ref, resid, out_ref, c * per, per)
        copy = pltpu.make_async_copy(
            out_ref.at[pl.ds(c * per, per)], result_ref.at[pl.ds(c * per, per), 0], sems.at[c]
        )
        copy.start()
        copies.append(copy)
    for copy in copies:
        copy.wait()


def on_device(
    inverse,
    start,
    source,
    mass,
    inner_elem,
    inner_face,
    inner_orient,
    inner_jac,
    cross_elem,
    cross_face,
    cross_orient,
    cross_count,
    cross_jac,
):
    size, elems = start.shape[1:]
    count_mesh = lax.axis_size("mesh")
    times = lax.axis_size("tm")
    half_times = times // 2
    cap = cross_elem.shape[1] // 5
    faces = inner_elem.shape[1]
    f32, i32, bf16 = jnp.float32, jnp.int32, jnp.bfloat16

    def struct(shape, dtype=f32):
        return jax.ShapeDtypeStruct(shape, dtype)

    state = struct((size, elems))
    near_shape = struct((72, 128))
    hot_cross = struct((6 * elems, 256), bf16)
    params = pltpu.CompilerParams(vmem_limit_bytes=16 * 1024 * 1024)
    dma = pltpu.SemaphoreType.DMA
    cost = pl.CostEstimate(flops=4000000000, bytes_accessed=1000000, transcendentals=0)

    across = [(t, (t + half_times) % times) for t in range(times)]
    halves = [list(range(half_times)), list(range(half_times, times))]
    evens = [(p, p ^ 1) for p in range(count_mesh)]
    odds = [(p, (((p + 1) ^ 1) - 1) % count_mesh) for p in range(count_mesh)]
    opposite = [(p, (p + count_mesh // 2) % count_mesh) for p in range(count_mesh)]

    start_rows = start.transpose(1, 0, 2)
    over = lax.ppermute(start_rows, "tm", across)
    x, near, far, send_hot = pl.pallas_call(
        first_kernel,
        out_shape=(state, near_shape, near_shape, hot_cross),
        in_specs=[HBM] * 3,
        out_specs=(VMEM,) * 4,
        scratch_shapes=[
            pltpu.VMEM(cross_elem.shape, i32),
            pltpu.VMEM(cross_face.shape, i32),
            dma((3,)),
        ],
        compiler_params=params,
    )(start_rows, cross_elem, cross_face)
    even = lax.ppermute(near, "mesh", evens)
    odd = lax.ppermute(near, "mesh", odds)
    jac_rows = inner_jac.transpose(0, 2, 1, 3)
    cross_rows = cross_jac[0]
    prepare = pl.pallas_call(
        functools.partial(prepare_kernel, cap),
        out_shape=(
            struct((216, elems)),
            struct((6 * elems, 2 * faces), bf16),
            struct((1, 2 * faces), i32),
            struct((40, 2 * faces)),
            hot_cross,
            struct((1, 256), i32),
            struct((40, 256)),
            state,
            state,
        ),
        in_specs=[VMEM] + [HBM] * 11,
        out_specs=(VMEM,) * 9,
        scratch_shapes=[
            pltpu.VMEM(inner_elem.shape, i32),
            pltpu.VMEM(inner_face.shape, i32),
            pltpu.VMEM((1, faces), i32),
            pltpu.VMEM(jac_rows.shape, f32),
            pltpu.VMEM(cross_elem.shape, i32),
            pltpu.VMEM(cross_face.shape, i32),
            pltpu.VMEM(cross_orient.shape, i32),
            pltpu.VMEM(cross_count.shape, i32),
            pltpu.VMEM(cross_rows.shape, f32),
            dma((11,)),
        ],
        compiler_params=params,
        cost_estimate=cost,
    )
    for sweep in range(SWEEPS):
        last = sweep == SWEEPS - 1
        if sweep > 0:
            over = lax.ppermute(x, "tm", across)
            even = lax.ppermute(near, "mesh", evens)
            odd = lax.ppermute(near, "mesh", odds)
        passed = pl.pallas_call(
            functools.partial(relay_kernel, cap),
            out_shape=near_shape,
            in_specs=[VMEM] * 3,
            out_specs=VMEM,
            compiler_params=params,
        )(even, odd, far)
        over, _ = lax.optimization_barrier((over, passed))
        terms = pl.pallas_call(
            functools.partial(combine_kernel, times),
            out_shape=struct((half_times, size, elems)),
            in_specs=[VMEM] * 2,
            out_specs=VMEM,
            compiler_params=params,
            cost_estimate=cost,
        )(x, over)
        passed = lax.ppermute(passed, "mesh", opposite)
        x, _ = lax.optimization_barrier((x, terms))
        if sweep > 0:
            inner = pl.pallas_call(
                inner_kernel,
                out_shape=struct((216, elems)),
                in_specs=[VMEM] * 4,
                out_specs=VMEM,
                compiler_params=params,
                cost_estimate=cost,
            )(x, hot, turn, jac)
        else:
            inner, hot, turn, jac, *tables = prepare(
                x,
                inner_elem,
                inner_face,
                inner_orient[None, :],
                jac_rows,
                cross_elem,
                cross_face,
                cross_orient,
                cross_count,
                cross_rows,
                source.transpose(1, 0, 2),
                mass,
            )
        terms = lax.all_to_all(
            terms, "tm", split_axis=0, concat_axis=0, tiled=True, axis_index_groups=halves
        )
        operands = (inner, even, odd, passed, *tables, terms, inverse)
        if last:
            out = pl.pallas_call(
                functools.partial(last_kernel, cap),
                out_shape=struct((size, 1, elems)),
                in_specs=[VMEM] * 11,
                out_specs=HBM,
                scratch_shapes=[
                    pltpu.VMEM((size, elems), f32),
                    pltpu.VMEM((size, elems), f32),
                    dma((3,)),
                ],
                compiler_params=params,
            )(*operands)
            return out.transpose(1, 0, 2)
        x, near, far = pl.pallas_call(
            functools.partial(middle_kernel, cap),
            out_shape=(state, near_shape, near_shape),
            in_specs=[VMEM] * 12,
            out_specs=(VMEM,) * 3,
            scratch_shapes=[pltpu.VMEM((size, elems), f32)],
            compiler_params=params,
        )(*operands, send_hot)


def solution(mesh):
    in_specs = (
        P("tm", None, None, "mesh"),
        P("tm", None, "mesh"),
        P("tm", None, "mesh"),
        P(None, "mesh"),
        P(None, "mesh"),
        P(None, "mesh"),
        P("mesh"),
        P("tm", None, None, "mesh"),
        P("mesh", None),
        P("mesh", None),
        P("mesh", None),
        P("mesh", None),
        P("tm", None, "mesh", None),
    )
    out_specs = P("tm", None, "mesh")
    return jax.shard_map(
        on_device, mesh=mesh, in_specs=in_specs, out_specs=out_specs, check_vma=False
    )
```

```python
import functools
import math

import jax
import jax.numpy as jnp
import numpy as np
from jax import lax
from jax.experimental import pallas as pl
from jax.experimental.pallas import tpu as pltpu
from jax.sharding import PartitionSpec as P

SWEEPS = 2
LINE = (1.0 / 3.0, 4.0 / 3.0, 1.0 / 3.0)
VMEM = pl.BlockSpec(memory_space=pltpu.VMEM)
HBM = pl.BlockSpec(memory_space=pltpu.HBM)


def face_node(face, n):
    normal = face // 2
    tangent = [axis for axis in range(3) if axis != normal]
    coords = [0, 0, 0]
    coords[normal] = 2 * (face % 2)
    coords[tangent[0]] = n % 3
    coords[tangent[1]] = n // 3
    return 9 * coords[2] + 3 * coords[1] + coords[0]


NODE = [[face_node(face, n) for n in range(9)] for face in range(6)]
WEIGHT = [float(np.float32(LINE[n % 3] * LINE[n // 3])) for n in range(9)]


def coef_table(times):
    table = [0.0] * times
    for k in range(1, times):
        sign = (-1.0) ** k
        phase = math.pi * k / times
        table[k] = float(
            np.float32(0.3 * sign * math.cos(phase) / math.sin(phase) + 1.2 * sign / times)
        )
    return table


def split_rows(value):
    high = value.astype(jnp.bfloat16).astype(jnp.float32)
    return jnp.concatenate([high, value - high], axis=0).astype(jnp.bfloat16)


def join_rows(value):
    half = value.shape[0] // 2
    return value[:half] + value[half:]


def face_rows(x_ref):
    elems = x_ref.shape[1]
    pad = jnp.zeros((3, elems), jnp.float32)
    nodes = [
        jnp.concatenate([x_ref[pl.ds(m, 5, stride=27), :], pad], axis=0) for m in range(27)
    ]
    blocks = []
    for face in range(6):
        rows = jnp.concatenate([nodes[NODE[face][n]] * WEIGHT[n] for n in range(9)], axis=0)
        blocks.append(split_rows(rows))
    return jnp.concatenate(blocks, axis=1)


def onehot(code, elems):
    slots = code.shape[1]
    row = lax.broadcasted_iota(jnp.int32, (elems, slots), 0)
    parts = [
        jnp.where(row == code - face * elems, 1.0, 0.0).astype(jnp.bfloat16) for face in range(6)
    ]
    return jnp.concatenate(parts, axis=0)


def cross_code(elem_ref, face_ref, elems, order):
    code = face_ref[...] * elems + elem_ref[...]
    cap = code.shape[1] // 5
    parts = [code[:, k * cap : (k + 1) * cap] for k in order]
    fill = 256 - code.shape[1]
    return jnp.concatenate(parts + [jnp.full((1, fill), -1, jnp.int32)], axis=1)


def cross_trace(x_ref, hot, near_ref, far_ref):
    trace = join_rows(jnp.dot(face_rows(x_ref), hot, preferred_element_type=jnp.float32))
    near_ref[...] = trace[:, :128]
    far_ref[...] = trace[:, 128:]


def fetch(pairs, sems):
    copies = [
        pltpu.make_async_copy(source, target, sems.at[i])
        for i, (source, target) in enumerate(pairs)
    ]
    for copy in copies:
        copy.start()
    return copies


def tick_kernel(out_ref):
    out_ref[...] = jnp.zeros_like(out_ref)


def mark_kernel(x_ref, out_ref):
    out_ref[...] = x_ref[:8]


def first_kernel(
    tick_ref, start_ref, elem_hbm, face_hbm, x_ref, near_ref, far_ref, hot_ref, elem_ref, face_ref, sems
):
    copies = fetch(
        ((start_ref.at[:, 0], x_ref), (elem_hbm, elem_ref), (face_hbm, face_ref)), sems
    )
    for copy in copies[1:]:
        copy.wait()
    elems = x_ref.shape[1]
    hot_ref[...] = onehot(cross_code(elem_ref, face_ref, elems, (0, 4, 1, 2, 3)), elems)
    copies[0].wait()
    cross_trace(x_ref, hot_ref[...], near_ref, far_ref)


def received_rows(trace, orient, jacobian):
    slots = trace.shape[1]
    code = jnp.broadcast_to(orient, (8, slots))
    flip_i = (code & 1) == 1
    flip_j = ((code >> 1) & 1) == 1
    swap = code >= 4
    tile = [trace[8 * n : 8 * n + 8] for n in range(9)]
    for j in range(3):
        low, high = tile[3 * j], tile[3 * j + 2]
        tile[3 * j] = jnp.where(flip_i, high, low)
        tile[3 * j + 2] = jnp.where(flip_i, low, high)
    for i in range(3):
        low, high = tile[i], tile[6 + i]
        tile[i] = jnp.where(flip_j, high, low)
        tile[6 + i] = jnp.where(flip_j, low, high)
    for j in range(3):
        for i in range(j):
            one, two = tile[3 * j + i], tile[3 * i + j]
            tile[3 * j + i] = jnp.where(swap, two, one)
            tile[3 * i + j] = jnp.where(swap, one, two)
    rows = []
    for n in range(9):
        total = jacobian[0] * tile[n][0:1]
        for u in range(1, 5):
            total = total + jacobian[u] * tile[n][u : u + 1]
        rows.append(total)
    return jnp.concatenate(rows, axis=0)


def scatter_nodes(rows, hot, elems):
    placed = join_rows(
        lax.dot_general(
            split_rows(rows), hot, (((1,), (1,)), ((), ())), preferred_element_type=jnp.float32
        )
    )
    nodes = [None] * 27
    for face in range(6):
        for n in range(9):
            part = placed[8 * n : 8 * n + 8, face * elems : (face + 1) * elems]
            m = NODE[face][n]
            nodes[m] = part if nodes[m] is None else nodes[m] + part
    return nodes


def inner_sum(x_ref, hot, orient, jac_ref, out_ref):
    elems = x_ref.shape[1]
    half = hot.shape[1] // 2
    trace = join_rows(jnp.dot(face_rows(x_ref), hot, preferred_element_type=jnp.float32))
    trace = jnp.concatenate([trace[:, half:], trace[:, :half]], axis=1)
    jacobian = [jac_ref[8 * u : 8 * u + 8, :] for u in range(5)]
    nodes = scatter_nodes(received_rows(trace, orient, jacobian), hot, elems)
    for m in range(27):
        out_ref[8 * m : 8 * m + 8, :] = (
            nodes[m] if nodes[m] is not None else jnp.zeros((8, elems), jnp.float32)
        )


def prepare_kernel(
    cap,
    x_ref,
    elem_hbm,
    face_hbm,
    orient_hbm,
    jac_hbm,
    cross_elem_hbm,
    cross_face_hbm,
    cross_orient_hbm,
    count_hbm,
    cross_jac_hbm,
    source_hbm,
    mass_hbm,
    out_ref,
    hot_ref,
    turn_ref,
    jac_ref,
    cross_hot_ref,
    cross_turn_ref,
    cross_jac_ref,
    source_ref,
    mass_ref,
    elem_ref,
    face_ref,
    orient_ref,
    raw_ref,
    cross_elem_ref,
    cross_face_ref,
    cross_orient_ref,
    count_ref,
    cross_raw_ref,
    sems,
):
    copies = fetch(
        (
            (elem_hbm, elem_ref),
            (face_hbm, face_ref),
            (orient_hbm, orient_ref),
            (jac_hbm, raw_ref),
            (cross_elem_hbm, cross_elem_ref),
            (cross_face_hbm, cross_face_ref),
            (cross_orient_hbm, cross_orient_ref),
            (count_hbm, count_ref),
            (cross_jac_hbm, cross_raw_ref),
            (source_hbm.at[:, 0], source_ref),
            (mass_hbm, mass_ref),
        ),
        sems,
    )
    for copy in copies:
        copy.wait()
    elems = x_ref.shape[1]
    half = elem_ref.shape[1]
    code = face_ref[...] * elems + elem_ref[...]
    hot_ref[...] = onehot(jnp.concatenate([code[0:1], code[1:2]], axis=1), elems)
    orient = orient_ref[...]
    back = jnp.where(orient >= 4, 4 + 2 * (orient & 1) + ((orient >> 1) & 1), orient)
    turn_ref[...] = jnp.concatenate([orient, back], axis=1)
    jac_ref[...] = jnp.zeros_like(jac_ref)
    for u in range(5):
        for v in range(5):
            for side in range(2):
                jac_ref[8 * u + v : 8 * u + v + 1, side * half : (side + 1) * half] = raw_ref[
                    0, 5 * u + v, side : side + 1, :
                ]
    slots = 5 * cap
    fill = 256 - slots
    cross_hot_ref[...] = onehot(
        cross_code(cross_elem_ref, cross_face_ref, elems, range(5)), elems
    )
    cross_turn_ref[...] = jnp.concatenate(
        [cross_orient_ref[...], jnp.zeros((1, fill), jnp.int32)], axis=1
    )
    lane = lax.broadcasted_iota(jnp.int32, (1, slots), 1)
    count = count_ref[...]
    live = lane < 0
    for k in range(5):
        live = live | ((lane >= k * cap) & (lane - k * cap < count[:, k : k + 1]))
    cross_jac_ref[...] = jnp.zeros_like(cross_jac_ref)
    for u in range(5):
        for v in range(5):
            row = cross_raw_ref[5 * u + v]
            cross_jac_ref[8 * u + v : 8 * u + v + 1, :slots] = jnp.where(live, row, 0.0)
    inner_sum(x_ref, hot_ref[...], turn_ref[...], jac_ref, out_ref)


def inner_kernel(x_ref, hot_ref, turn_ref, jac_ref, out_ref):
    inner_sum(x_ref, hot_ref[...], turn_ref[...], jac_ref, out_ref)


def combine_kernel(times, x_ref, z_ref, out_ref):
    table = coef_table(times)
    half = times // 2
    y = lax.axis_index("tm") % half
    x = x_ref[...]
    z = z_ref[...] if len(z_ref.shape) == 2 else z_ref[:, 0, :]
    for target in range(half):
        own = jnp.float32(0.0)
        other = jnp.float32(0.0)
        for at in range(half):
            own = jnp.where(y == at, table[(at - target) % times], own)
            other = jnp.where(y == at, table[(at - target + half) % times], other)
        out_ref[target] = x * own + z * other


def relay_kernel(cap, even_ref, odd_ref, near_ref, far_ref, out_ref):
    part = lax.axis_index("mesh")
    half = lax.axis_size("mesh") // 2
    is_even = part % 2 == 0
    even = even_ref[...]
    odd = odd_ref[...]
    above = jnp.where(is_even, even, odd)
    below = jnp.where(is_even, odd, even)
    one = jnp.where(
        part % half == 0, near_ref[:, 2 * cap : 3 * cap], below[:, cap : 2 * cap]
    )
    two = jnp.where(
        part % half == half - 1, near_ref[:, :cap], above[:, 3 * cap : 4 * cap]
    )
    out_ref[...] = jnp.concatenate([far_ref[:, :cap], one, two, two], axis=1)


def forward_kernel(cap, near_ref, far_ref, out_ref):
    out_ref[...] = jnp.concatenate(
        [
            near_ref[:, cap : 2 * cap],
            near_ref[:, 3 * cap : 4 * cap],
            far_ref[:, cap : 2 * cap],
            far_ref[:, 2 * cap : 3 * cap],
        ],
        axis=1,
    )


def solve(held_ref, resid, out_ref, first, count):
    def body(step, carry):
        for r in range(5):
            i = first + step * 5 + r
            product = held_ref[0, i].astype(jnp.float32) * resid
            out_ref[pl.ds(i, 1), :] = jnp.sum(product, axis=0, keepdims=True)
        return carry

    lax.fori_loop(0, count // 5, body, 0)


def residual(
    cap,
    inner_ref,
    even_ref,
    odd_ref,
    far_ref,
    edge_ref,
    hot_ref,
    turn_ref,
    jac_ref,
    source_ref,
    mass_ref,
    terms_ref,
    resid_ref,
):
    elems = source_ref.shape[1]
    part = lax.axis_index("mesh")
    half = lax.axis_size("mesh") // 2
    is_even = part % 2 == 0
    first = part % half == 0
    final = part % half == half - 1
    even = even_ref[...]
    odd = odd_ref[...]
    far = far_ref[...]
    edge = edge_ref[...]
    above = jnp.where(is_even, even, odd)
    below = jnp.where(is_even, odd, even)
    trace = jnp.concatenate(
        [
            jnp.where(final, edge[:, 2 * cap : 3 * cap], above[:, 2 * cap : 3 * cap]),
            jnp.where(first, edge[:, 3 * cap : 4 * cap], below[:, :cap]),
            jnp.where(first, edge[:, :cap], far[:, cap : 2 * cap]),
            far[:, :cap],
            jnp.where(final, edge[:, cap : 2 * cap], far[:, 2 * cap : 3 * cap]),
            jnp.zeros((72, 256 - 5 * cap), jnp.float32),
        ],
        axis=1,
    )
    jacobian = [jac_ref[8 * u : 8 * u + 8, :] for u in range(5)]
    nodes = scatter_nodes(received_rows(trace, turn_ref[...], jacobian), hot_ref[...], elems)
    for m in range(27):
        part = inner_ref[8 * m : 8 * m + 8, :]
        part = part if nodes[m] is None else part + nodes[m]
        resid_ref[pl.ds(m, 5, stride=27), :] = part[:5]
    spectral = (terms_ref[0] + terms_ref[1]) + (terms_ref[2] + terms_ref[3])
    resid = source_ref[...] - resid_ref[...] - mass_ref[...] * spectral
    return resid.astype(jnp.bfloat16).astype(jnp.float32)


def middle_kernel(cap, *refs):
    *operands, held_ref, send_ref, out_ref, near_ref, far_ref, resid_ref = refs
    resid = residual(cap, *operands, resid_ref)
    solve(held_ref, resid, out_ref, 0, held_ref.shape[1])
    cross_trace(out_ref, send_ref[...], near_ref, far_ref)


def last_kernel(cap, *refs):
    *operands, held_ref, result_ref, resid_ref, out_ref, sems = refs
    resid = residual(cap, *operands, resid_ref)
    per = held_ref.shape[1] // 3
    copies = []
    for c in range(3):
        solve(held_ref, resid, out_ref, c * per, per)
        copy = pltpu.make_async_copy(
            out_ref.at[pl.ds(c * per, per)], result_ref.at[pl.ds(c * per, per), 0], sems.at[c]
        )
        copy.start()
        copies.append(copy)
    for copy in copies:
        copy.wait()


def on_device(
    inverse,
    start,
    source,
    mass,
    inner_elem,
    inner_face,
    inner_orient,
    inner_jac,
    cross_elem,
    cross_face,
    cross_orient,
    cross_count,
    cross_jac,
):
    size, elems = start.shape[1:]
    count_mesh = lax.axis_size("mesh")
    times = lax.axis_size("tm")
    half_times = times // 2
    cap = cross_elem.shape[1] // 5
    faces = inner_elem.shape[1]
    f32, i32, bf16 = jnp.float32, jnp.int32, jnp.bfloat16

    def struct(shape, dtype=f32):
        return jax.ShapeDtypeStruct(shape, dtype)

    state = struct((size, elems))
    near_shape = struct((72, 128))
    hot_cross = struct((6 * elems, 256), bf16)
    params = pltpu.CompilerParams(vmem_limit_bytes=16 * 1024 * 1024)
    dma = pltpu.SemaphoreType.DMA
    cost = pl.CostEstimate(flops=4000000000, bytes_accessed=1000000, transcendentals=0)

    across = [(t, (t + half_times) % times) for t in range(times)]
    halves = [list(range(half_times)), list(range(half_times, times))]
    evens = [(p, p ^ 1) for p in range(count_mesh)]
    half_mesh = count_mesh // 2
    odds = [
        (p, ((p + 1) ^ 1) - 1)
        for p in range(count_mesh)
        if p % half_mesh not in (0, half_mesh - 1)
    ]
    edges = [
        (p, p // half_mesh * half_mesh + half_mesh - 1 - p % half_mesh)
        for p in range(count_mesh)
        if p % half_mesh in (0, half_mesh - 1)
    ]
    opposite = [(p, (p + count_mesh // 2) % count_mesh) for p in range(count_mesh)]

    start_rows = start.transpose(1, 0, 2)
    tick = pl.pallas_call(
        tick_kernel,
        out_shape=struct((8, 128)),
        out_specs=VMEM,
        compiler_params=params,
        cost_estimate=cost,
    )()
    sent, tick = lax.optimization_barrier((start_rows, tick))
    over = lax.ppermute(sent, "tm", across)
    x, near, far, send_hot = pl.pallas_call(
        first_kernel,
        out_shape=(state, near_shape, near_shape, hot_cross),
        in_specs=[VMEM] + [HBM] * 3,
        out_specs=(VMEM,) * 4,
        scratch_shapes=[
            pltpu.VMEM(cross_elem.shape, i32),
            pltpu.VMEM(cross_face.shape, i32),
            dma((3,)),
        ],
        compiler_params=params,
    )(tick, start_rows, cross_elem, cross_face)
    even = lax.ppermute(near, "mesh", evens)
    odd = lax.ppermute(near, "mesh", odds)
    jac_rows = inner_jac.transpose(0, 2, 1, 3)
    cross_rows = cross_jac[0]
    prepare = pl.pallas_call(
        functools.partial(prepare_kernel, cap),
        out_shape=(
            struct((216, elems)),
            struct((6 * elems, 2 * faces), bf16),
            struct((1, 2 * faces), i32),
            struct((40, 2 * faces)),
            hot_cross,
            struct((1, 256), i32),
            struct((40, 256)),
            state,
            state,
        ),
        in_specs=[VMEM] + [HBM] * 11,
        out_specs=(VMEM,) * 9,
        scratch_shapes=[
            pltpu.VMEM(inner_elem.shape, i32),
            pltpu.VMEM(inner_face.shape, i32),
            pltpu.VMEM((1, faces), i32),
            pltpu.VMEM(jac_rows.shape, f32),
            pltpu.VMEM(cross_elem.shape, i32),
            pltpu.VMEM(cross_face.shape, i32),
            pltpu.VMEM(cross_orient.shape, i32),
            pltpu.VMEM(cross_count.shape, i32),
            pltpu.VMEM(cross_rows.shape, f32),
            dma((11,)),
        ],
        compiler_params=params,
        cost_estimate=cost,
    )
    for sweep in range(SWEEPS):
        last = sweep == SWEEPS - 1
        if sweep > 0:
            over = lax.ppermute(x, "tm", across)
            even = lax.ppermute(near, "mesh", evens)
            odd = lax.ppermute(near, "mesh", odds)
        passed = pl.pallas_call(
            functools.partial(relay_kernel, cap),
            out_shape=near_shape,
            in_specs=[VMEM] * 4,
            out_specs=VMEM,
            compiler_params=params,
        )(even, odd, near, far)
        over, _ = lax.optimization_barrier((over, passed))
        terms = pl.pallas_call(
            functools.partial(combine_kernel, times),
            out_shape=struct((half_times, size, elems)),
            in_specs=[VMEM] * 2,
            out_specs=VMEM,
            compiler_params=params,
            cost_estimate=cost,
        )(x, over)
        passed = lax.ppermute(passed, "mesh", opposite)
        x, _ = lax.optimization_barrier((x, terms))
        beside = pl.pallas_call(
            mark_kernel,
            out_shape=struct((8, 128)),
            in_specs=[VMEM],
            out_specs=VMEM,
            compiler_params=params,
            cost_estimate=cost,
        )(x)
        passed, _ = lax.optimization_barrier((passed, beside))
        edge = pl.pallas_call(
            functools.partial(forward_kernel, cap),
            out_shape=near_shape,
            in_specs=[VMEM] * 2,
            out_specs=VMEM,
            compiler_params=params,
        )(near, passed)
        x, edge = lax.optimization_barrier((x, edge))
        edge = lax.ppermute(edge, "mesh", edges)
        if sweep > 0:
            inner = pl.pallas_call(
                inner_kernel,
                out_shape=struct((216, elems)),
                in_specs=[VMEM] * 4,
                out_specs=VMEM,
                compiler_params=params,
                cost_estimate=cost,
            )(x, hot, turn, jac)
        else:
            inner, hot, turn, jac, *tables = prepare(
                x,
                inner_elem,
                inner_face,
                inner_orient[None, :],
                jac_rows,
                cross_elem,
                cross_face,
                cross_orient,
                cross_count,
                cross_rows,
                source.transpose(1, 0, 2),
                mass,
            )
        terms = lax.all_to_all(
            terms, "tm", split_axis=0, concat_axis=0, tiled=True, axis_index_groups=halves
        )
        operands = (inner, even, odd, passed, edge, *tables, terms, inverse)
        if last:
            out = pl.pallas_call(
                functools.partial(last_kernel, cap),
                out_shape=struct((size, 1, elems)),
                in_specs=[VMEM] * 12,
                out_specs=HBM,
                scratch_shapes=[
                    pltpu.VMEM((size, elems), f32),
                    pltpu.VMEM((size, elems), f32),
                    dma((3,)),
                ],
                compiler_params=params,
            )(*operands)
            return out.transpose(1, 0, 2)
        x, near, far = pl.pallas_call(
            functools.partial(middle_kernel, cap),
            out_shape=(state, near_shape, near_shape),
            in_specs=[VMEM] * 13,
            out_specs=(VMEM,) * 3,
            scratch_shapes=[pltpu.VMEM((size, elems), f32)],
            compiler_params=params,
        )(*operands, send_hot)


def solution(mesh):
    in_specs = (
        P("tm", None, None, "mesh"),
        P("tm", None, "mesh"),
        P("tm", None, "mesh"),
        P(None, "mesh"),
        P(None, "mesh"),
        P(None, "mesh"),
        P("mesh"),
        P("tm", None, None, "mesh"),
        P("mesh", None),
        P("mesh", None),
        P("mesh", None),
        P("mesh", None),
        P("tm", None, "mesh", None),
    )
    out_specs = P("tm", None, "mesh")
    return jax.shard_map(
        on_device, mesh=mesh, in_specs=in_specs, out_specs=out_specs, check_vma=False
    )
```

```python
import functools
import math

import jax
import jax.numpy as jnp
import numpy as np
from jax import lax
from jax.experimental import pallas as pl
from jax.experimental.pallas import tpu as pltpu
from jax.sharding import PartitionSpec as P

SWEEPS = 2
LINE = (1.0 / 3.0, 4.0 / 3.0, 1.0 / 3.0)
VMEM = pl.BlockSpec(memory_space=pltpu.VMEM)
HBM = pl.BlockSpec(memory_space=pltpu.HBM)


def face_node(face, n):
    normal = face // 2
    tangent = [axis for axis in range(3) if axis != normal]
    coords = [0, 0, 0]
    coords[normal] = 2 * (face % 2)
    coords[tangent[0]] = n % 3
    coords[tangent[1]] = n // 3
    return 9 * coords[2] + 3 * coords[1] + coords[0]


NODE = [[face_node(face, n) for n in range(9)] for face in range(6)]
WEIGHT = [float(np.float32(LINE[n % 3] * LINE[n // 3])) for n in range(9)]


def coef_table(times):
    table = [0.0] * times
    for k in range(1, times):
        sign = (-1.0) ** k
        phase = math.pi * k / times
        table[k] = float(
            np.float32(0.3 * sign * math.cos(phase) / math.sin(phase) + 1.2 * sign / times)
        )
    return table


def split_rows(value):
    high = value.astype(jnp.bfloat16).astype(jnp.float32)
    return jnp.concatenate([high, value - high], axis=0).astype(jnp.bfloat16)


def join_rows(value):
    half = value.shape[0] // 2
    return value[:half] + value[half:]


def face_rows(x_ref):
    elems = x_ref.shape[1]
    pad = jnp.zeros((3, elems), jnp.float32)
    nodes = [
        jnp.concatenate([x_ref[pl.ds(m, 5, stride=27), :], pad], axis=0) for m in range(27)
    ]
    blocks = []
    for face in range(6):
        rows = jnp.concatenate([nodes[NODE[face][n]] * WEIGHT[n] for n in range(9)], axis=0)
        blocks.append(split_rows(rows))
    return jnp.concatenate(blocks, axis=1)


def onehot(code, elems):
    slots = code.shape[1]
    row = lax.broadcasted_iota(jnp.int32, (elems, slots), 0)
    parts = [
        jnp.where(row == code - face * elems, 1.0, 0.0).astype(jnp.bfloat16) for face in range(6)
    ]
    return jnp.concatenate(parts, axis=0)


def cross_code(elem_ref, face_ref, elems, order):
    code = face_ref[...] * elems + elem_ref[...]
    cap = code.shape[1] // 5
    parts = [code[:, k * cap : (k + 1) * cap] for k in order]
    fill = 256 - code.shape[1]
    return jnp.concatenate(parts + [jnp.full((1, fill), -1, jnp.int32)], axis=1)


def cross_trace(x_ref, hot, near_ref, far_ref):
    trace = join_rows(jnp.dot(face_rows(x_ref), hot, preferred_element_type=jnp.float32))
    near_ref[...] = trace[:, :128]
    far_ref[...] = trace[:, 128:]


def fetch(pairs, sems):
    copies = [
        pltpu.make_async_copy(source, target, sems.at[i])
        for i, (source, target) in enumerate(pairs)
    ]
    for copy in copies:
        copy.start()
    return copies


def tick_kernel(out_ref):
    out_ref[...] = jnp.zeros_like(out_ref)


def mark_kernel(x_ref, out_ref):
    out_ref[...] = x_ref[:8]


def first_kernel(
    tick_ref, start_ref, elem_hbm, face_hbm, x_ref, near_ref, far_ref, hot_ref, elem_ref, face_ref, sems
):
    copies = fetch(
        ((start_ref.at[:, 0], x_ref), (elem_hbm, elem_ref), (face_hbm, face_ref)), sems
    )
    for copy in copies[1:]:
        copy.wait()
    elems = x_ref.shape[1]
    hot_ref[...] = onehot(cross_code(elem_ref, face_ref, elems, (0, 4, 1, 2, 3)), elems)
    copies[0].wait()
    cross_trace(x_ref, hot_ref[...], near_ref, far_ref)


def received_rows(trace, orient, jacobian):
    slots = trace.shape[1]
    code = jnp.broadcast_to(orient, (8, slots))
    flip_i = (code & 1) == 1
    flip_j = ((code >> 1) & 1) == 1
    swap = code >= 4
    tile = [trace[8 * n : 8 * n + 8] for n in range(9)]
    for j in range(3):
        low, high = tile[3 * j], tile[3 * j + 2]
        tile[3 * j] = jnp.where(flip_i, high, low)
        tile[3 * j + 2] = jnp.where(flip_i, low, high)
    for i in range(3):
        low, high = tile[i], tile[6 + i]
        tile[i] = jnp.where(flip_j, high, low)
        tile[6 + i] = jnp.where(flip_j, low, high)
    for j in range(3):
        for i in range(j):
            one, two = tile[3 * j + i], tile[3 * i + j]
            tile[3 * j + i] = jnp.where(swap, two, one)
            tile[3 * i + j] = jnp.where(swap, one, two)
    rows = []
    for n in range(9):
        total = jacobian[0] * tile[n][0:1]
        for u in range(1, 5):
            total = total + jacobian[u] * tile[n][u : u + 1]
        rows.append(total)
    return jnp.concatenate(rows, axis=0)


def scatter_nodes(rows, hot, elems):
    placed = join_rows(
        lax.dot_general(
            split_rows(rows), hot, (((1,), (1,)), ((), ())), preferred_element_type=jnp.float32
        )
    )
    nodes = [None] * 27
    for face in range(6):
        for n in range(9):
            part = placed[8 * n : 8 * n + 8, face * elems : (face + 1) * elems]
            m = NODE[face][n]
            nodes[m] = part if nodes[m] is None else nodes[m] + part
    return nodes


def inner_sum(x_ref, hot, orient, jac_ref, out_ref):
    elems = x_ref.shape[1]
    half = hot.shape[1] // 2
    trace = join_rows(jnp.dot(face_rows(x_ref), hot, preferred_element_type=jnp.float32))
    trace = jnp.concatenate([trace[:, half:], trace[:, :half]], axis=1)
    jacobian = [jac_ref[8 * u : 8 * u + 8, :] for u in range(5)]
    nodes = scatter_nodes(received_rows(trace, orient, jacobian), hot, elems)
    for m in range(27):
        out_ref[8 * m : 8 * m + 8, :] = (
            nodes[m] if nodes[m] is not None else jnp.zeros((8, elems), jnp.float32)
        )


def prepare_kernel(
    cap,
    x_ref,
    elem_hbm,
    face_hbm,
    orient_hbm,
    jac_hbm,
    cross_elem_hbm,
    cross_face_hbm,
    cross_orient_hbm,
    count_hbm,
    cross_jac_hbm,
    source_hbm,
    mass_hbm,
    out_ref,
    hot_ref,
    turn_ref,
    jac_ref,
    cross_hot_ref,
    cross_turn_ref,
    cross_jac_ref,
    source_ref,
    mass_ref,
    elem_ref,
    face_ref,
    orient_ref,
    raw_ref,
    cross_elem_ref,
    cross_face_ref,
    cross_orient_ref,
    count_ref,
    cross_raw_ref,
    sems,
):
    copies = fetch(
        (
            (elem_hbm, elem_ref),
            (face_hbm, face_ref),
            (orient_hbm, orient_ref),
            (jac_hbm, raw_ref),
            (cross_elem_hbm, cross_elem_ref),
            (cross_face_hbm, cross_face_ref),
            (cross_orient_hbm, cross_orient_ref),
            (count_hbm, count_ref),
            (cross_jac_hbm, cross_raw_ref),
            (source_hbm.at[:, 0], source_ref),
            (mass_hbm, mass_ref),
        ),
        sems,
    )
    for copy in copies:
        copy.wait()
    elems = x_ref.shape[1]
    half = elem_ref.shape[1]
    code = face_ref[...] * elems + elem_ref[...]
    hot_ref[...] = onehot(jnp.concatenate([code[0:1], code[1:2]], axis=1), elems)
    orient = orient_ref[...]
    back = jnp.where(orient >= 4, 4 + 2 * (orient & 1) + ((orient >> 1) & 1), orient)
    turn_ref[...] = jnp.concatenate([orient, back], axis=1)
    jac_ref[...] = jnp.zeros_like(jac_ref)
    for u in range(5):
        for v in range(5):
            for side in range(2):
                jac_ref[8 * u + v : 8 * u + v + 1, side * half : (side + 1) * half] = raw_ref[
                    0, 5 * u + v, side : side + 1, :
                ]
    slots = 5 * cap
    fill = 256 - slots
    cross_hot_ref[...] = onehot(
        cross_code(cross_elem_ref, cross_face_ref, elems, range(5)), elems
    )
    cross_turn_ref[...] = jnp.concatenate(
        [cross_orient_ref[...], jnp.zeros((1, fill), jnp.int32)], axis=1
    )
    lane = lax.broadcasted_iota(jnp.int32, (1, slots), 1)
    count = count_ref[...]
    live = lane < 0
    for k in range(5):
        live = live | ((lane >= k * cap) & (lane - k * cap < count[:, k : k + 1]))
    cross_jac_ref[...] = jnp.zeros_like(cross_jac_ref)
    for u in range(5):
        for v in range(5):
            row = cross_raw_ref[5 * u + v]
            cross_jac_ref[8 * u + v : 8 * u + v + 1, :slots] = jnp.where(live, row, 0.0)
    inner_sum(x_ref, hot_ref[...], turn_ref[...], jac_ref, out_ref)


def inner_kernel(x_ref, hot_ref, turn_ref, jac_ref, out_ref):
    inner_sum(x_ref, hot_ref[...], turn_ref[...], jac_ref, out_ref)


def combine_kernel(times, x_ref, z_ref, out_ref):
    table = coef_table(times)
    half = times // 2
    y = lax.axis_index("tm") % half
    x = x_ref[...]
    z = z_ref[...] if len(z_ref.shape) == 2 else z_ref[:, 0, :]
    for target in range(half):
        own = jnp.float32(0.0)
        other = jnp.float32(0.0)
        for at in range(half):
            own = jnp.where(y == at, table[(at - target) % times], own)
            other = jnp.where(y == at, table[(at - target + half) % times], other)
        out_ref[target] = x * own + z * other


def relay_kernel(cap, even_ref, odd_ref, near_ref, far_ref, out_ref):
    part = lax.axis_index("mesh")
    half = lax.axis_size("mesh") // 2
    is_even = part % 2 == 0
    even = even_ref[...]
    odd = odd_ref[...]
    above = jnp.where(is_even, even, odd)
    below = jnp.where(is_even, odd, even)
    one = jnp.where(
        part % half == 0, near_ref[:, 2 * cap : 3 * cap], below[:, cap : 2 * cap]
    )
    two = jnp.where(
        part % half == half - 1, near_ref[:, :cap], above[:, 3 * cap : 4 * cap]
    )
    out_ref[...] = jnp.concatenate([far_ref[:, :cap], one, two, two], axis=1)


def forward_kernel(cap, near_ref, far_ref, out_ref):
    out_ref[...] = jnp.concatenate(
        [
            near_ref[:, cap : 2 * cap],
            near_ref[:, 3 * cap : 4 * cap],
            far_ref[:, cap : 2 * cap],
            far_ref[:, 2 * cap : 3 * cap],
        ],
        axis=1,
    )


def solve(held_ref, resid, out_ref, first, count):
    def body(step, carry):
        for r in range(5):
            i = first + step * 5 + r
            product = held_ref[0, i].astype(jnp.float32) * resid
            out_ref[pl.ds(i, 1), :] = jnp.sum(product, axis=0, keepdims=True)
        return carry

    lax.fori_loop(0, count // 5, body, 0)


def residual(
    cap,
    inner_ref,
    even_ref,
    odd_ref,
    far_ref,
    edge_ref,
    hot_ref,
    turn_ref,
    jac_ref,
    source_ref,
    mass_ref,
    terms_ref,
    resid_ref,
):
    elems = source_ref.shape[1]
    part = lax.axis_index("mesh")
    half = lax.axis_size("mesh") // 2
    is_even = part % 2 == 0
    first = part % half == 0
    final = part % half == half - 1
    even = even_ref[...]
    odd = odd_ref[...]
    far = far_ref[...]
    edge = edge_ref[...]
    above = jnp.where(is_even, even, odd)
    below = jnp.where(is_even, odd, even)
    trace = jnp.concatenate(
        [
            jnp.where(final, edge[:, 2 * cap : 3 * cap], above[:, 2 * cap : 3 * cap]),
            jnp.where(first, edge[:, 3 * cap : 4 * cap], below[:, :cap]),
            jnp.where(first, edge[:, :cap], far[:, cap : 2 * cap]),
            far[:, :cap],
            jnp.where(final, edge[:, cap : 2 * cap], far[:, 2 * cap : 3 * cap]),
            jnp.zeros((72, 256 - 5 * cap), jnp.float32),
        ],
        axis=1,
    )
    jacobian = [jac_ref[8 * u : 8 * u + 8, :] for u in range(5)]
    nodes = scatter_nodes(received_rows(trace, turn_ref[...], jacobian), hot_ref[...], elems)
    for m in range(27):
        part = inner_ref[8 * m : 8 * m + 8, :]
        part = part if nodes[m] is None else part + nodes[m]
        resid_ref[pl.ds(m, 5, stride=27), :] = part[:5]
    spectral = (terms_ref[0] + terms_ref[1]) + (terms_ref[2] + terms_ref[3])
    resid = source_ref[...] - resid_ref[...] - mass_ref[...] * spectral
    return resid.astype(jnp.bfloat16).astype(jnp.float32)


def residual_kernel(cap, *refs):
    *operands, out_ref, sum_ref = refs
    out_ref[...] = residual(cap, *operands, sum_ref)


def middle_kernel(resid_ref, held_ref, send_ref, out_ref, near_ref, far_ref):
    solve(held_ref, resid_ref[...], out_ref, 0, held_ref.shape[1])
    cross_trace(out_ref, send_ref[...], near_ref, far_ref)


def last_kernel(resid_ref, held_ref, result_ref, out_ref, sems):
    resid = resid_ref[...]
    per = held_ref.shape[1] // 3
    copies = []
    for c in range(3):
        solve(held_ref, resid, out_ref, c * per, per)
        copy = pltpu.make_async_copy(
            out_ref.at[pl.ds(c * per, per)], result_ref.at[pl.ds(c * per, per), 0], sems.at[c]
        )
        copy.start()
        copies.append(copy)
    for copy in copies:
        copy.wait()


def on_device(
    inverse,
    start,
    source,
    mass,
    inner_elem,
    inner_face,
    inner_orient,
    inner_jac,
    cross_elem,
    cross_face,
    cross_orient,
    cross_count,
    cross_jac,
):
    size, elems = start.shape[1:]
    count_mesh = lax.axis_size("mesh")
    times = lax.axis_size("tm")
    half_times = times // 2
    cap = cross_elem.shape[1] // 5
    faces = inner_elem.shape[1]
    f32, i32, bf16 = jnp.float32, jnp.int32, jnp.bfloat16

    def struct(shape, dtype=f32):
        return jax.ShapeDtypeStruct(shape, dtype)

    state = struct((size, elems))
    near_shape = struct((72, 128))
    hot_cross = struct((6 * elems, 256), bf16)
    params = pltpu.CompilerParams(vmem_limit_bytes=16 * 1024 * 1024)
    dma = pltpu.SemaphoreType.DMA
    cost = pl.CostEstimate(flops=4000000000, bytes_accessed=1000000, transcendentals=0)

    across = [(t, (t + half_times) % times) for t in range(times)]
    halves = [list(range(half_times)), list(range(half_times, times))]
    evens = [(p, p ^ 1) for p in range(count_mesh)]
    half_mesh = count_mesh // 2
    odds = [
        (p, ((p + 1) ^ 1) - 1)
        for p in range(count_mesh)
        if p % half_mesh not in (0, half_mesh - 1)
    ]
    edges = [
        (p, p // half_mesh * half_mesh + half_mesh - 1 - p % half_mesh)
        for p in range(count_mesh)
        if p % half_mesh in (0, half_mesh - 1)
    ]
    opposite = [(p, (p + count_mesh // 2) % count_mesh) for p in range(count_mesh)]

    start_rows = start.transpose(1, 0, 2)
    tick = pl.pallas_call(
        tick_kernel,
        out_shape=struct((8, 128)),
        out_specs=VMEM,
        compiler_params=params,
        cost_estimate=cost,
    )()
    sent, tick = lax.optimization_barrier((start_rows, tick))
    over = lax.ppermute(sent, "tm", across)
    x, near, far, send_hot = pl.pallas_call(
        first_kernel,
        out_shape=(state, near_shape, near_shape, hot_cross),
        in_specs=[VMEM] + [HBM] * 3,
        out_specs=(VMEM,) * 4,
        scratch_shapes=[
            pltpu.VMEM(cross_elem.shape, i32),
            pltpu.VMEM(cross_face.shape, i32),
            dma((3,)),
        ],
        compiler_params=params,
    )(tick, start_rows, cross_elem, cross_face)
    even = lax.ppermute(near, "mesh", evens)
    odd = lax.ppermute(near, "mesh", odds)
    jac_rows = inner_jac.transpose(0, 2, 1, 3)
    cross_rows = cross_jac[0]
    prepare = pl.pallas_call(
        functools.partial(prepare_kernel, cap),
        out_shape=(
            struct((216, elems)),
            struct((6 * elems, 2 * faces), bf16),
            struct((1, 2 * faces), i32),
            struct((40, 2 * faces)),
            hot_cross,
            struct((1, 256), i32),
            struct((40, 256)),
            state,
            state,
        ),
        in_specs=[VMEM] + [HBM] * 11,
        out_specs=(VMEM,) * 9,
        scratch_shapes=[
            pltpu.VMEM(inner_elem.shape, i32),
            pltpu.VMEM(inner_face.shape, i32),
            pltpu.VMEM((1, faces), i32),
            pltpu.VMEM(jac_rows.shape, f32),
            pltpu.VMEM(cross_elem.shape, i32),
            pltpu.VMEM(cross_face.shape, i32),
            pltpu.VMEM(cross_orient.shape, i32),
            pltpu.VMEM(cross_count.shape, i32),
            pltpu.VMEM(cross_rows.shape, f32),
            dma((11,)),
        ],
        compiler_params=params,
        cost_estimate=cost,
    )
    for sweep in range(SWEEPS):
        last = sweep == SWEEPS - 1
        if sweep > 0:
            over = lax.ppermute(x, "tm", across)
            even = lax.ppermute(near, "mesh", evens)
            odd = lax.ppermute(near, "mesh", odds)
        passed = pl.pallas_call(
            functools.partial(relay_kernel, cap),
            out_shape=near_shape,
            in_specs=[VMEM] * 4,
            out_specs=VMEM,
            compiler_params=params,
        )(even, odd, near, far)
        over, _ = lax.optimization_barrier((over, passed))
        terms = pl.pallas_call(
            functools.partial(combine_kernel, times),
            out_shape=struct((half_times, size, elems)),
            in_specs=[VMEM] * 2,
            out_specs=VMEM,
            compiler_params=params,
            cost_estimate=cost,
        )(x, over)
        passed = lax.ppermute(passed, "mesh", opposite)
        x, _ = lax.optimization_barrier((x, terms))
        beside = pl.pallas_call(
            mark_kernel,
            out_shape=struct((8, 128)),
            in_specs=[VMEM],
            out_specs=VMEM,
            compiler_params=params,
            cost_estimate=cost,
        )(x)
        passed, _ = lax.optimization_barrier((passed, beside))
        edge = pl.pallas_call(
            functools.partial(forward_kernel, cap),
            out_shape=near_shape,
            in_specs=[VMEM] * 2,
            out_specs=VMEM,
            compiler_params=params,
        )(near, passed)
        x, edge = lax.optimization_barrier((x, edge))
        edge = lax.ppermute(edge, "mesh", edges)
        if sweep > 0:
            inner = pl.pallas_call(
                inner_kernel,
                out_shape=struct((216, elems)),
                in_specs=[VMEM] * 4,
                out_specs=VMEM,
                compiler_params=params,
                cost_estimate=cost,
            )(x, hot, turn, jac)
        else:
            inner, hot, turn, jac, *tables = prepare(
                x,
                inner_elem,
                inner_face,
                inner_orient[None, :],
                jac_rows,
                cross_elem,
                cross_face,
                cross_orient,
                cross_count,
                cross_rows,
                source.transpose(1, 0, 2),
                mass,
            )
        terms = lax.all_to_all(
            terms, "tm", split_axis=0, concat_axis=0, tiled=True, axis_index_groups=halves
        )
        resid = pl.pallas_call(
            functools.partial(residual_kernel, cap),
            out_shape=state,
            in_specs=[VMEM] * 11,
            out_specs=VMEM,
            scratch_shapes=[pltpu.VMEM((size, elems), f32)],
            compiler_params=params,
            cost_estimate=cost,
        )(inner, even, odd, passed, edge, *tables, terms)
        if last:
            out = pl.pallas_call(
                last_kernel,
                out_shape=struct((size, 1, elems)),
                in_specs=[VMEM] * 2,
                out_specs=HBM,
                scratch_shapes=[pltpu.VMEM((size, elems), f32), dma((3,))],
                compiler_params=params,
            )(resid, inverse)
            return out.transpose(1, 0, 2)
        x, near, far = pl.pallas_call(
            middle_kernel,
            out_shape=(state, near_shape, near_shape),
            in_specs=[VMEM] * 3,
            out_specs=(VMEM,) * 3,
            compiler_params=params,
        )(resid, inverse, send_hot)


def solution(mesh):
    in_specs = (
        P("tm", None, None, "mesh"),
        P("tm", None, "mesh"),
        P("tm", None, "mesh"),
        P(None, "mesh"),
        P(None, "mesh"),
        P(None, "mesh"),
        P("mesh"),
        P("tm", None, None, "mesh"),
        P("mesh", None),
        P("mesh", None),
        P("mesh", None),
        P("mesh", None),
        P("tm", None, "mesh", None),
    )
    out_specs = P("tm", None, "mesh")
    return jax.shard_map(
        on_device, mesh=mesh, in_specs=in_specs, out_specs=out_specs, check_vma=False
    )
```

```python
import functools
import math

import jax
import jax.numpy as jnp
import numpy as np
from jax import lax
from jax.experimental import pallas as pl
from jax.experimental.pallas import tpu as pltpu
from jax.sharding import PartitionSpec as P

SWEEPS = 2
LINE = (1.0 / 3.0, 4.0 / 3.0, 1.0 / 3.0)
VMEM = pl.BlockSpec(memory_space=pltpu.VMEM)
HBM = pl.BlockSpec(memory_space=pltpu.HBM)


def face_node(face, n):
    normal = face // 2
    tangent = [axis for axis in range(3) if axis != normal]
    coords = [0, 0, 0]
    coords[normal] = 2 * (face % 2)
    coords[tangent[0]] = n % 3
    coords[tangent[1]] = n // 3
    return 9 * coords[2] + 3 * coords[1] + coords[0]


NODE = [[face_node(face, n) for n in range(9)] for face in range(6)]
WEIGHT = [float(np.float32(LINE[n % 3] * LINE[n // 3])) for n in range(9)]


def coef_table(times):
    table = [0.0] * times
    for k in range(1, times):
        sign = (-1.0) ** k
        phase = math.pi * k / times
        table[k] = float(
            np.float32(0.3 * sign * math.cos(phase) / math.sin(phase) + 1.2 * sign / times)
        )
    return table


def split_rows(value):
    high = value.astype(jnp.bfloat16).astype(jnp.float32)
    return jnp.concatenate([high, value - high], axis=0).astype(jnp.bfloat16)


def join_rows(value):
    half = value.shape[0] // 2
    return value[:half] + value[half:]


def face_rows(x_ref):
    elems = x_ref.shape[1]
    pad = jnp.zeros((3, elems), jnp.float32)
    nodes = [
        jnp.concatenate([x_ref[pl.ds(m, 5, stride=27), :], pad], axis=0) for m in range(27)
    ]
    blocks = []
    for face in range(6):
        rows = jnp.concatenate([nodes[NODE[face][n]] * WEIGHT[n] for n in range(9)], axis=0)
        blocks.append(split_rows(rows))
    return jnp.concatenate(blocks, axis=1)


def onehot(code, elems):
    slots = code.shape[1]
    row = lax.broadcasted_iota(jnp.int32, (elems, slots), 0)
    parts = [
        jnp.where(row == code - face * elems, 1.0, 0.0).astype(jnp.bfloat16) for face in range(6)
    ]
    return jnp.concatenate(parts, axis=0)


def cross_code(elem_ref, face_ref, elems, order):
    code = face_ref[...] * elems + elem_ref[...]
    cap = code.shape[1] // 5
    parts = [code[:, k * cap : (k + 1) * cap] for k in order]
    fill = 256 - code.shape[1]
    return jnp.concatenate(parts + [jnp.full((1, fill), -1, jnp.int32)], axis=1)


def cross_trace(x_ref, hot, near_ref, far_ref):
    trace = join_rows(jnp.dot(face_rows(x_ref), hot, preferred_element_type=jnp.float32))
    near_ref[...] = trace[:, :128]
    far_ref[...] = trace[:, 128:]


def fetch(pairs, sems):
    copies = [
        pltpu.make_async_copy(source, target, sems.at[i])
        for i, (source, target) in enumerate(pairs)
    ]
    for copy in copies:
        copy.start()
    return copies


def tick_kernel(out_ref):
    out_ref[...] = jnp.zeros_like(out_ref)


def mark_kernel(x_ref, out_ref):
    out_ref[...] = x_ref[:8]


def first_kernel(
    tick_ref, start_ref, elem_hbm, face_hbm, x_ref, near_ref, far_ref, hot_ref, elem_ref, face_ref, sems
):
    copies = fetch(
        ((start_ref.at[:, 0], x_ref), (elem_hbm, elem_ref), (face_hbm, face_ref)), sems
    )
    for copy in copies[1:]:
        copy.wait()
    elems = x_ref.shape[1]
    hot_ref[...] = onehot(cross_code(elem_ref, face_ref, elems, (0, 4, 1, 2, 3)), elems)
    copies[0].wait()
    cross_trace(x_ref, hot_ref[...], near_ref, far_ref)


def received_rows(trace, orient, jacobian):
    slots = trace.shape[1]
    code = jnp.broadcast_to(orient, (8, slots))
    flip_i = (code & 1) == 1
    flip_j = ((code >> 1) & 1) == 1
    swap = code >= 4
    tile = [trace[8 * n : 8 * n + 8] for n in range(9)]
    for j in range(3):
        low, high = tile[3 * j], tile[3 * j + 2]
        tile[3 * j] = jnp.where(flip_i, high, low)
        tile[3 * j + 2] = jnp.where(flip_i, low, high)
    for i in range(3):
        low, high = tile[i], tile[6 + i]
        tile[i] = jnp.where(flip_j, high, low)
        tile[6 + i] = jnp.where(flip_j, low, high)
    for j in range(3):
        for i in range(j):
            one, two = tile[3 * j + i], tile[3 * i + j]
            tile[3 * j + i] = jnp.where(swap, two, one)
            tile[3 * i + j] = jnp.where(swap, one, two)
    rows = []
    for n in range(9):
        total = jacobian[0] * tile[n][0:1]
        for u in range(1, 5):
            total = total + jacobian[u] * tile[n][u : u + 1]
        rows.append(total)
    return jnp.concatenate(rows, axis=0)


def scatter_nodes(rows, hot, elems):
    placed = join_rows(
        lax.dot_general(
            split_rows(rows), hot, (((1,), (1,)), ((), ())), preferred_element_type=jnp.float32
        )
    )
    nodes = [None] * 27
    for face in range(6):
        for n in range(9):
            part = placed[8 * n : 8 * n + 8, face * elems : (face + 1) * elems]
            m = NODE[face][n]
            nodes[m] = part if nodes[m] is None else nodes[m] + part
    return nodes


def inner_sum(x_ref, hot, orient, jac_ref, out_ref):
    elems = x_ref.shape[1]
    half = hot.shape[1] // 2
    trace = join_rows(jnp.dot(face_rows(x_ref), hot, preferred_element_type=jnp.float32))
    trace = jnp.concatenate([trace[:, half:], trace[:, :half]], axis=1)
    jacobian = [jac_ref[8 * u : 8 * u + 8, :] for u in range(5)]
    nodes = scatter_nodes(received_rows(trace, orient, jacobian), hot, elems)
    for m in range(27):
        out_ref[8 * m : 8 * m + 8, :] = (
            nodes[m] if nodes[m] is not None else jnp.zeros((8, elems), jnp.float32)
        )


def prepare_kernel(
    cap,
    x_ref,
    elem_hbm,
    face_hbm,
    orient_hbm,
    jac_hbm,
    cross_elem_hbm,
    cross_face_hbm,
    cross_orient_hbm,
    count_hbm,
    cross_jac_hbm,
    source_hbm,
    mass_hbm,
    out_ref,
    hot_ref,
    turn_ref,
    jac_ref,
    cross_hot_ref,
    cross_turn_ref,
    cross_jac_ref,
    source_ref,
    mass_ref,
    elem_ref,
    face_ref,
    orient_ref,
    raw_ref,
    cross_elem_ref,
    cross_face_ref,
    cross_orient_ref,
    count_ref,
    cross_raw_ref,
    sems,
):
    copies = fetch(
        (
            (elem_hbm, elem_ref),
            (face_hbm, face_ref),
            (orient_hbm, orient_ref),
            (jac_hbm, raw_ref),
            (cross_elem_hbm, cross_elem_ref),
            (cross_face_hbm, cross_face_ref),
            (cross_orient_hbm, cross_orient_ref),
            (count_hbm, count_ref),
            (cross_jac_hbm, cross_raw_ref),
            (source_hbm.at[:, 0], source_ref),
            (mass_hbm, mass_ref),
        ),
        sems,
    )
    for copy in copies:
        copy.wait()
    elems = x_ref.shape[1]
    half = elem_ref.shape[1]
    code = face_ref[...] * elems + elem_ref[...]
    hot_ref[...] = onehot(jnp.concatenate([code[0:1], code[1:2]], axis=1), elems)
    orient = orient_ref[...]
    back = jnp.where(orient >= 4, 4 + 2 * (orient & 1) + ((orient >> 1) & 1), orient)
    turn_ref[...] = jnp.concatenate([orient, back], axis=1)
    jac_ref[...] = jnp.zeros_like(jac_ref)
    for u in range(5):
        for v in range(5):
            for side in range(2):
                jac_ref[8 * u + v : 8 * u + v + 1, side * half : (side + 1) * half] = raw_ref[
                    0, 5 * u + v, side : side + 1, :
                ]
    slots = 5 * cap
    fill = 256 - slots
    cross_hot_ref[...] = onehot(
        cross_code(cross_elem_ref, cross_face_ref, elems, range(5)), elems
    )
    cross_turn_ref[...] = jnp.concatenate(
        [cross_orient_ref[...], jnp.zeros((1, fill), jnp.int32)], axis=1
    )
    lane = lax.broadcasted_iota(jnp.int32, (1, slots), 1)
    count = count_ref[...]
    live = lane < 0
    for k in range(5):
        live = live | ((lane >= k * cap) & (lane - k * cap < count[:, k : k + 1]))
    cross_jac_ref[...] = jnp.zeros_like(cross_jac_ref)
    for u in range(5):
        for v in range(5):
            row = cross_raw_ref[5 * u + v]
            cross_jac_ref[8 * u + v : 8 * u + v + 1, :slots] = jnp.where(live, row, 0.0)
    inner_sum(x_ref, hot_ref[...], turn_ref[...], jac_ref, out_ref)


def inner_kernel(x_ref, hot_ref, turn_ref, jac_ref, out_ref):
    inner_sum(x_ref, hot_ref[...], turn_ref[...], jac_ref, out_ref)


def combine_kernel(times, x_ref, z_ref, out_ref):
    table = coef_table(times)
    half = times // 2
    y = lax.axis_index("tm") % half
    x = x_ref[...]
    z = z_ref[...] if len(z_ref.shape) == 2 else z_ref[:, 0, :]
    for target in range(half):
        own = jnp.float32(0.0)
        other = jnp.float32(0.0)
        for at in range(half):
            own = jnp.where(y == at, table[(at - target) % times], own)
            other = jnp.where(y == at, table[(at - target + half) % times], other)
        out_ref[target] = x * own + z * other


def relay_kernel(cap, even_ref, odd_ref, near_ref, far_ref, out_ref):
    part = lax.axis_index("mesh")
    half = lax.axis_size("mesh") // 2
    is_even = part % 2 == 0
    even = even_ref[...]
    odd = odd_ref[...]
    above = jnp.where(is_even, even, odd)
    below = jnp.where(is_even, odd, even)
    one = jnp.where(
        part % half == 0, near_ref[:, 2 * cap : 3 * cap], below[:, cap : 2 * cap]
    )
    two = jnp.where(
        part % half == half - 1, near_ref[:, :cap], above[:, 3 * cap : 4 * cap]
    )
    out_ref[...] = jnp.concatenate([far_ref[:, :cap], one, two, two], axis=1)


def forward_kernel(cap, near_ref, far_ref, out_ref):
    out_ref[...] = jnp.concatenate(
        [
            near_ref[:, cap : 2 * cap],
            near_ref[:, 3 * cap : 4 * cap],
            far_ref[:, cap : 2 * cap],
            far_ref[:, 2 * cap : 3 * cap],
        ],
        axis=1,
    )


def solve(held_ref, resid, out_ref, first, count):
    def body(step, carry):
        for r in range(5):
            i = first + step * 5 + r
            product = held_ref[0, i].astype(jnp.float32) * resid
            out_ref[pl.ds(i, 1), :] = jnp.sum(product, axis=0, keepdims=True)
        return carry

    lax.fori_loop(0, count // 5, body, 0)


def residual(
    cap,
    inner_ref,
    even_ref,
    odd_ref,
    far_ref,
    edge_ref,
    hot_ref,
    turn_ref,
    jac_ref,
    source_ref,
    mass_ref,
    terms_ref,
    resid_ref,
):
    elems = source_ref.shape[1]
    part = lax.axis_index("mesh")
    half = lax.axis_size("mesh") // 2
    is_even = part % 2 == 0
    first = part % half == 0
    final = part % half == half - 1
    even = even_ref[...]
    odd = odd_ref[...]
    far = far_ref[...]
    edge = edge_ref[...]
    above = jnp.where(is_even, even, odd)
    below = jnp.where(is_even, odd, even)
    trace = jnp.concatenate(
        [
            jnp.where(final, edge[:, 2 * cap : 3 * cap], above[:, 2 * cap : 3 * cap]),
            jnp.where(first, edge[:, 3 * cap : 4 * cap], below[:, :cap]),
            jnp.where(first, edge[:, :cap], far[:, cap : 2 * cap]),
            far[:, :cap],
            jnp.where(final, edge[:, cap : 2 * cap], far[:, 2 * cap : 3 * cap]),
            jnp.zeros((72, 256 - 5 * cap), jnp.float32),
        ],
        axis=1,
    )
    jacobian = [jac_ref[8 * u : 8 * u + 8, :] for u in range(5)]
    nodes = scatter_nodes(received_rows(trace, turn_ref[...], jacobian), hot_ref[...], elems)
    for m in range(27):
        part = inner_ref[8 * m : 8 * m + 8, :]
        part = part if nodes[m] is None else part + nodes[m]
        resid_ref[pl.ds(m, 5, stride=27), :] = part[:5]
    spectral = (terms_ref[0] + terms_ref[1]) + (terms_ref[2] + terms_ref[3])
    resid = source_ref[...] - resid_ref[...] - mass_ref[...] * spectral
    return resid.astype(jnp.bfloat16).astype(jnp.float32)


def residual_kernel(cap, *refs):
    *operands, out_ref, sum_ref = refs
    out_ref[...] = residual(cap, *operands, sum_ref)


def middle_kernel(resid_ref, held_ref, send_ref, out_ref, near_ref, far_ref):
    solve(held_ref, resid_ref[...], out_ref, 0, held_ref.shape[1])
    cross_trace(out_ref, send_ref[...], near_ref, far_ref)


def last_kernel(resid_ref, held_ref, result_ref, out_ref, sems):
    resid = resid_ref[...]
    per = held_ref.shape[1] // 3
    copies = []
    for c in range(3):
        solve(held_ref, resid, out_ref, c * per, per)
        copy = pltpu.make_async_copy(
            out_ref.at[pl.ds(c * per, per)], result_ref.at[pl.ds(c * per, per), 0], sems.at[c]
        )
        copy.start()
        copies.append(copy)
    for copy in copies:
        copy.wait()


def on_device(
    inverse,
    start,
    source,
    mass,
    inner_elem,
    inner_face,
    inner_orient,
    inner_jac,
    cross_elem,
    cross_face,
    cross_orient,
    cross_count,
    cross_jac,
):
    size, elems = start.shape[1:]
    count_mesh = lax.axis_size("mesh")
    times = lax.axis_size("tm")
    half_times = times // 2
    cap = cross_elem.shape[1] // 5
    faces = inner_elem.shape[1]
    f32, i32, bf16 = jnp.float32, jnp.int32, jnp.bfloat16

    def struct(shape, dtype=f32):
        return jax.ShapeDtypeStruct(shape, dtype)

    state = struct((size, elems))
    near_shape = struct((72, 128))
    hot_cross = struct((6 * elems, 256), bf16)
    params = pltpu.CompilerParams(vmem_limit_bytes=16 * 1024 * 1024)
    dma = pltpu.SemaphoreType.DMA
    cost = pl.CostEstimate(flops=4000000000, bytes_accessed=1000000, transcendentals=0)

    across = [(t, (t + half_times) % times) for t in range(times)]
    halves = [list(range(half_times)), list(range(half_times, times))]
    evens = [(p, p ^ 1) for p in range(count_mesh)]
    half_mesh = count_mesh // 2
    odds = [
        (p, ((p + 1) ^ 1) - 1)
        for p in range(count_mesh)
        if p % half_mesh not in (0, half_mesh - 1)
    ]
    edges = [
        (p, p // half_mesh * half_mesh + half_mesh - 1 - p % half_mesh)
        for p in range(count_mesh)
        if p % half_mesh in (0, half_mesh - 1)
    ]
    opposite = [(p, (p + count_mesh // 2) % count_mesh) for p in range(count_mesh)]

    start_rows = start.transpose(1, 0, 2)
    tick = pl.pallas_call(
        tick_kernel,
        out_shape=struct((8, 128)),
        out_specs=VMEM,
        compiler_params=params,
        cost_estimate=cost,
    )()
    sent, tick = lax.optimization_barrier((start_rows, tick))
    over = lax.ppermute(sent, "tm", across)
    x, near, far, send_hot = pl.pallas_call(
        first_kernel,
        out_shape=(state, near_shape, near_shape, hot_cross),
        in_specs=[VMEM] + [HBM] * 3,
        out_specs=(VMEM,) * 4,
        scratch_shapes=[
            pltpu.VMEM(cross_elem.shape, i32),
            pltpu.VMEM(cross_face.shape, i32),
            dma((3,)),
        ],
        compiler_params=params,
    )(tick, start_rows, cross_elem, cross_face)
    odd = lax.ppermute(near, "mesh", odds)
    even = lax.ppermute(near, "mesh", evens)
    jac_rows = inner_jac.transpose(0, 2, 1, 3)
    cross_rows = cross_jac[0]
    prepare = pl.pallas_call(
        functools.partial(prepare_kernel, cap),
        out_shape=(
            struct((216, elems)),
            struct((6 * elems, 2 * faces), bf16),
            struct((1, 2 * faces), i32),
            struct((40, 2 * faces)),
            hot_cross,
            struct((1, 256), i32),
            struct((40, 256)),
            state,
            state,
        ),
        in_specs=[VMEM] + [HBM] * 11,
        out_specs=(VMEM,) * 9,
        scratch_shapes=[
            pltpu.VMEM(inner_elem.shape, i32),
            pltpu.VMEM(inner_face.shape, i32),
            pltpu.VMEM((1, faces), i32),
            pltpu.VMEM(jac_rows.shape, f32),
            pltpu.VMEM(cross_elem.shape, i32),
            pltpu.VMEM(cross_face.shape, i32),
            pltpu.VMEM(cross_orient.shape, i32),
            pltpu.VMEM(cross_count.shape, i32),
            pltpu.VMEM(cross_rows.shape, f32),
            dma((11,)),
        ],
        compiler_params=params,
        cost_estimate=cost,
    )
    for sweep in range(SWEEPS):
        last = sweep == SWEEPS - 1
        if sweep > 0:
            over = lax.ppermute(x, "tm", across)
            odd = lax.ppermute(near, "mesh", odds)
            even = lax.ppermute(near, "mesh", evens)
        passed = pl.pallas_call(
            functools.partial(relay_kernel, cap),
            out_shape=near_shape,
            in_specs=[VMEM] * 4,
            out_specs=VMEM,
            compiler_params=params,
        )(even, odd, near, far)
        over, _ = lax.optimization_barrier((over, passed))
        terms = pl.pallas_call(
            functools.partial(combine_kernel, times),
            out_shape=struct((half_times, size, elems)),
            in_specs=[VMEM] * 2,
            out_specs=VMEM,
            compiler_params=params,
            cost_estimate=cost,
        )(x, over)
        passed = lax.ppermute(passed, "mesh", opposite)
        x, _ = lax.optimization_barrier((x, terms))
        beside = pl.pallas_call(
            mark_kernel,
            out_shape=struct((8, 128)),
            in_specs=[VMEM],
            out_specs=VMEM,
            compiler_params=params,
            cost_estimate=cost,
        )(x)
        passed, _ = lax.optimization_barrier((passed, beside))
        edge = pl.pallas_call(
            functools.partial(forward_kernel, cap),
            out_shape=near_shape,
            in_specs=[VMEM] * 2,
            out_specs=VMEM,
            compiler_params=params,
        )(near, passed)
        x, edge = lax.optimization_barrier((x, edge))
        edge = lax.ppermute(edge, "mesh", edges)
        if sweep > 0:
            inner = pl.pallas_call(
                inner_kernel,
                out_shape=struct((216, elems)),
                in_specs=[VMEM] * 4,
                out_specs=VMEM,
                compiler_params=params,
                cost_estimate=cost,
            )(x, hot, turn, jac)
        else:
            inner, hot, turn, jac, *tables = prepare(
                x,
                inner_elem,
                inner_face,
                inner_orient[None, :],
                jac_rows,
                cross_elem,
                cross_face,
                cross_orient,
                cross_count,
                cross_rows,
                source.transpose(1, 0, 2),
                mass,
            )
        terms = lax.all_to_all(
            terms, "tm", split_axis=0, concat_axis=0, tiled=True, axis_index_groups=halves
        )
        resid = pl.pallas_call(
            functools.partial(residual_kernel, cap),
            out_shape=state,
            in_specs=[VMEM] * 11,
            out_specs=VMEM,
            scratch_shapes=[pltpu.VMEM((size, elems), f32)],
            compiler_params=params,
            cost_estimate=cost,
        )(inner, even, odd, passed, edge, *tables, terms)
        if last:
            out = pl.pallas_call(
                last_kernel,
                out_shape=struct((size, 1, elems)),
                in_specs=[VMEM] * 2,
                out_specs=HBM,
                scratch_shapes=[pltpu.VMEM((size, elems), f32), dma((3,))],
                compiler_params=params,
            )(resid, inverse)
            return out.transpose(1, 0, 2)
        x, near, far = pl.pallas_call(
            middle_kernel,
            out_shape=(state, near_shape, near_shape),
            in_specs=[VMEM] * 3,
            out_specs=(VMEM,) * 3,
            compiler_params=params,
        )(resid, inverse, send_hot)


def solution(mesh):
    in_specs = (
        P("tm", None, None, "mesh"),
        P("tm", None, "mesh"),
        P("tm", None, "mesh"),
        P(None, "mesh"),
        P(None, "mesh"),
        P(None, "mesh"),
        P("mesh"),
        P("tm", None, None, "mesh"),
        P("mesh", None),
        P("mesh", None),
        P("mesh", None),
        P("mesh", None),
        P("tm", None, "mesh", None),
    )
    out_specs = P("tm", None, "mesh")
    return jax.shard_map(
        on_device, mesh=mesh, in_specs=in_specs, out_specs=out_specs, check_vma=False
    )
```
